32 devices in a mesh: pipe: 2 (over x), expert: 4 (over y, core), edp: 4 (over z).
Axes of the slice: x: 2, y: 2, z: 4, core: 2. Of those that a mesh axis runs over, the one named last changes fastest.
Arguments:
- head_grads: bfloat16 [2, 1024, 1792], P('pipe', ('expert', 'edp')), may hold values from -6 to 6
- tail_grad: bfloat16 [1024, 1792], P(('expert', 'edp')), may hold values from -6 to 6
- saved_input: bfloat16 [2, 2, 1024, 1792], P('pipe', None, ('expert', 'edp')), may hold values from -48 to 48
- norm_gain: float32 [2, 1792], P('pipe'), may hold values from 0.25 to 1.75
- route_expert: int32 [2, 2, 1024, 1], P('pipe', None, ('expert', 'edp')), may hold values from 0 to 3, as said below
- route_slot: int32 [2, 2, 1024, 1], P('pipe', None, ('expert', 'edp')), may hold values from 0 to 15, as said below
- gates: float32 [2, 2, 1024, 1], P('pipe', None, ('expert', 'edp')), may hold values from 0.05 to 0.6
- saved_pre: bfloat16 [2, 2, 4, 256, 1408], P('pipe', None, 'expert', 'edp'), may hold values from -6 to 6
- w_gate_up: bfloat16 [2, 4, 1792, 1408], P('pipe', 'expert'), may hold values from -0.125 to 0.125
- w_down: bfloat16 [2, 4, 704, 1792], P('pipe', 'expert'), may hold values from -0.21875 to 0.21875
Outputs:
- input_grads: bfloat16 [2, 2, 1024, 1792], P('pipe', None, ('expert', 'edp'))
- w_down_grad: float32 [2, 4, 704, 1792], P('pipe', 'expert', 'edp')
The draws below stay inside these ranges and needn't reach their ends.
Inputs may be any that keep to these rules, and one draw needn't show every extreme that they name: `route_expert`: for each section, round and block of 64 consecutive tokens, each token names 1 different experts and each expert is named exactly 16 times; the experts fall into 1 disjoint sets of 4, and a token's k-th choice lies in the k-th set. `route_slot`: within one such block, the choices that name one expert carry the slots 0 to 15, each once.
All inputs are finite; a program needn't handle non-finite values.
Results may differ from the reference program's by a relative error of at most 0.0052.
Values may be sent and summed in bfloat16 or wider, within the bound.
No kernel may reach another device: no remote copies, remote signals or barrier semaphores. Data moves between devices by JAX's collectives and lax.ppermute only.
A program may use at most 64 MiB of HBM per device.

```python
import math
import jax
import jax.numpy as jnp
from jax import lax

D = 1792
FF = 704
TOPK = 1
ROUNDS = 2
TOK = 64
EXPERTS = 4
REPLICAS = 4
SECTIONS = 2
NTOK = 1024
CAP = 16
SLOTS = 256


def route_table(key):
    blocks = SECTIONS * ROUNDS * (NTOK // TOK)
    groups = EXPERTS // TOPK
    block_keys = jax.random.split(jax.random.fold_in(key, 7), blocks)

    def one_block(block_key):
        perm_key, label_key = jax.random.split(block_key)
        orders = jax.vmap(lambda subkey: jax.random.permutation(subkey, TOK))(jax.random.split(perm_key, TOPK))
        places = orders.T.astype(jnp.int32)
        offsets = jnp.arange(TOPK, dtype=jnp.int32)[None, :] * groups
        labels = jax.random.permutation(label_key, EXPERTS).astype(jnp.int32)
        chosen = labels[places // CAP + offsets]
        return (chosen, (places % CAP).astype(jnp.int32))
    chosen, slotted = jax.vmap(one_block)(block_keys)
    target_shape = (SECTIONS, ROUNDS, NTOK, TOPK)
    return (chosen.reshape(target_shape), slotted.reshape(target_shape))


def draw_route_expert(key, part):
    return route_table(key)[0]


def draw_route_slot(key, part):
    return route_table(key)[1]


def draw_saved_input(key, part):
    noise_key, row_key, column_key = jax.random.split(jax.random.fold_in(key, 11), 3)
    full_shape = (SECTIONS, ROUNDS, NTOK, D)
    noise = jnp.clip(jax.random.normal(noise_key, full_shape, jnp.float32), -4.0, 4.0)
    row_scale = jnp.exp(jax.random.uniform(row_key, (SECTIONS, ROUNDS, NTOK, 1), jnp.float32, math.log(0.3), math.log(3.0)))
    column_scale = jnp.exp(jax.random.uniform(column_key, (SECTIONS, ROUNDS, 1, D), jnp.float32, math.log(0.3), math.log(3.0)))
    return (noise * row_scale * column_scale).astype(jnp.bfloat16)


def steps_of(rng, shape, cuts, smallest, top_value):
    def one(dim, shards_of):
        steps = jax.random.uniform(jax.random.fold_in(jax.random.fold_in(rng, 6), dim), (shards_of,), jnp.float32, smallest / len(cuts), top_value / len(cuts))
        return jnp.repeat(jnp.exp(steps), shape[dim] // shards_of).reshape((-1,) + (1,) * (len(shape) - dim - 1))

    gain = one(*cuts[0])
    for cut in cuts[1:]:
        gain = gain * one(*cut)
    return gain


def bell_draw(key, dims, deviation, most, cuts=(), kind=jnp.bfloat16):
    level = steps_of(key, dims, cuts, -0.22, 0.18) if cuts else 1.0
    array = jax.random.normal(key, dims, jnp.float32) * deviation * level
    return jnp.minimum(jnp.maximum(array, -most), most).astype(kind)


def setup_inputs(seed: int = 0) -> dict:
    keys = jax.random.split(jax.random.key(seed), 11)
    head_grads = bell_draw(keys[0], (SECTIONS, NTOK, D), 1.0, 6.0, ((0, 2), (1, 16)))
    tail_grad = bell_draw(keys[1], (NTOK, D), 1.0, 6.0, ((0, 16),))
    saved_input = draw_saved_input(jax.random.fold_in(keys[10], 71), 0)
    norm_gain = jnp.clip(1.0 + 0.15 * jax.random.normal(keys[3], (SECTIONS, D), jnp.float32), 0.25, 1.75)
    route_expert = draw_route_expert(jax.random.fold_in(keys[10], 71), 0)
    route_slot = draw_route_slot(jax.random.fold_in(keys[10], 71), 0)
    gates = jnp.clip(jnp.exp(math.log(0.6) - 2.4849067 * jax.random.uniform(keys[6], (SECTIONS, ROUNDS, NTOK, TOPK), jnp.float32) ** steps_of(keys[6], (SECTIONS, ROUNDS, NTOK, TOPK), ((0, 2), (2, 16)), -0.2, 0.2)), 0.05, 0.6)
    saved_pre = bell_draw(keys[7], (SECTIONS, ROUNDS, EXPERTS, SLOTS, 2 * FF), 1.0, 6.0, ((0, 2), (2, 4), (3, 4)))
    w_gate_up = bell_draw(keys[8], (SECTIONS, EXPERTS, D, 2 * FF), D ** -0.5, 0.125, ((0, 2), (1, 4)))
    w_down = bell_draw(keys[9], (SECTIONS, EXPERTS, FF, D), FF ** -0.5, 0.21875, ((0, 2), (1, 4)))
    return dict(head_grads=head_grads, tail_grad=tail_grad, saved_input=saved_input, norm_gain=norm_gain, route_expert=route_expert, route_slot=route_slot, gates=gates, saved_pre=saved_pre, w_gate_up=w_gate_up, w_down=w_down)


norm_eps = 1e-06

def expert_pass(operands):
    routed, stored, gate_up, down = operands
    hidden_grad = jnp.dot(routed, down.T, preferred_element_type=jnp.float32)
    values = stored.astype(jnp.float32)
    gate_pre = values[:, :FF]
    up_value = values[:, FF:]
    sigmoid_gate = jax.nn.sigmoid(gate_pre)
    silu_gate = gate_pre * sigmoid_gate
    act_grad = jnp.concatenate([hidden_grad * up_value * sigmoid_gate * (1.0 + gate_pre * (1.0 - sigmoid_gate)), hidden_grad * silu_gate], axis=1).astype(jnp.bfloat16)
    expert_grad = jnp.dot(act_grad, gate_up.T, preferred_element_type=jnp.float32).astype(jnp.bfloat16)
    hidden = (silu_gate * up_value).astype(jnp.bfloat16)
    weight_term = jnp.dot(hidden.T, routed, preferred_element_type=jnp.float32)
    return (expert_grad, weight_term)

def layer_pass(grad_now, saved_now, gain_now, picked, placed, weights_now, stored, gate_up, down):
    tokens = grad_now.shape[0]
    blocks = jnp.arange(tokens, dtype=jnp.int32) // TOK
    base_rows = blocks % REPLICAS * (EXPERTS * CAP) + blocks // REPLICAS * CAP
    row_index = (base_rows[:, None] + placed).astype(jnp.int32)
    dispatched = jnp.zeros((EXPERTS, SLOTS, D), jnp.bfloat16)
    for slot_rank in range(TOPK):
        scaled = (grad_now.astype(jnp.float32) * weights_now[:, slot_rank][:, None]).astype(jnp.bfloat16)
        dispatched = dispatched.at[picked[:, slot_rank], row_index[:, slot_rank]].set(scaled)
    expert_grad, weight_terms = lax.map(expert_pass, (dispatched, stored, gate_up, down))
    branch = jnp.zeros((tokens, D), jnp.float32)
    for slot_rank in range(TOPK):
        branch = branch + expert_grad[picked[:, slot_rank], row_index[:, slot_rank]].astype(jnp.float32)
    normed_in = saved_now.astype(jnp.float32)
    inverse = lax.rsqrt(lax.optimization_barrier(jnp.mean(normed_in * normed_in, axis=1, keepdims=True)) + norm_eps)
    scaled_in = normed_in * inverse
    norm_grad = branch * gain_now[None, :].astype(jnp.float32)
    result = grad_now.astype(jnp.float32) + inverse * (norm_grad - scaled_in * lax.optimization_barrier(jnp.mean(norm_grad * scaled_in, axis=1, keepdims=True)))
    return (result.astype(jnp.bfloat16), weight_terms)

def reference(head_grads, tail_grad, saved_input, norm_gain, route_expert, route_slot, gates, saved_pre, w_gate_up, w_down):
    first_outs = []
    first_terms = []
    for section_index in range(SECTIONS):
        result, terms = layer_pass(head_grads[section_index], saved_input[section_index, 0], norm_gain[section_index], route_expert[section_index, 0], route_slot[section_index, 0], gates[section_index, 0], saved_pre[section_index, 0], w_gate_up[section_index], w_down[section_index])
        first_outs.append(result)
        first_terms.append(terms)
    second_outs = []
    grads_out = []
    for section_index in range(SECTIONS):
        if section_index == SECTIONS - 1:
            incoming = tail_grad
        else:
            incoming = first_outs[section_index + 1]
        result, terms = layer_pass(incoming, saved_input[section_index, 1], norm_gain[section_index], route_expert[section_index, 1], route_slot[section_index, 1], gates[section_index, 1], saved_pre[section_index, 1], w_gate_up[section_index], w_down[section_index])
        second_outs.append(result)
        grads_out.append((first_terms[section_index] + terms) / (REPLICAS * ROUNDS))
    input_grads = jnp.stack([jnp.stack([first_outs[section_index], second_outs[section_index]]) for section_index in range(SECTIONS)])
    w_down_grad = jnp.stack(grads_out)
    return (input_grads, w_down_grad)
```

```python
import jax
import jax.numpy as jnp
from jax import lax
from jax.experimental import pallas as pl
from jax.experimental.pallas import tpu as pltpu
from jax.sharding import PartitionSpec as P

ROUNDS = 2
NORM_EPS = 1e-06
VMEM_LIMIT = 24 * 2**20

bf16 = jnp.bfloat16
f32 = jnp.float32


def on_chip(body, outs, args, flops=0, moved=0):
    spec = pl.BlockSpec(memory_space=pltpu.VMEM)
    return pl.pallas_call(
        body,
        out_shape=outs,
        in_specs=[spec] * len(args),
        out_specs=jax.tree.map(lambda _: spec, outs),
        compiler_params=pltpu.CompilerParams(vmem_limit_bytes=VMEM_LIMIT),
        cost_estimate=pl.CostEstimate(flops=flops, bytes_accessed=moved, transcendentals=0),
    )(*args)


def dot(left, right, left_dim, right_dim):
    return lax.dot_general(
        left, right, (((left_dim,), (right_dim,)), ((), ())), preferred_element_type=f32
    )


def split_rows(value, refs, rows):
    for index, ref in enumerate(refs):
        ref[...] = value[index * rows : (index + 1) * rows].astype(ref.dtype)


def join_rows(refs):
    if len(refs) == 1:
        return refs[0][...]
    return jnp.concatenate([ref[...] for ref in refs], axis=0)


def one_hot(target, rows):
    lanes = lax.broadcasted_iota(jnp.int32, (target.shape[0], rows), 1)
    return jnp.where(target == lanes, 1.0, 0.0).astype(bf16)


def target_of(expert, slot, capacity):
    mine = lax.axis_index("expert")
    return (expert ^ mine) * capacity + slot


def dispatch_rows(grad, gate, target, rows):
    scaled = (grad.astype(f32) * gate).astype(bf16)
    return dot(one_hot(target, rows), scaled, 0, 0)


def stored_rows(stored_ref, round_index, senders, capacity):
    mine = lax.axis_index("expert")
    if capacity % 16 == 0:
        return jnp.concatenate(
            [
                stored_ref[
                    0,
                    round_index,
                    0,
                    pl.ds(pl.multiple_of((mine ^ step) * capacity, 16), capacity),
                    :,
                ]
                for step in range(senders)
            ],
            axis=0,
        ).astype(f32)
    rows = senders * capacity
    row = lax.broadcasted_iota(jnp.int32, (rows, rows), 0)
    column = lax.broadcasted_iota(jnp.int32, (rows, rows), 1)
    moved = ((row // capacity) ^ mine) * capacity + row % capacity
    order = jnp.where(moved == column, 1.0, 0.0).astype(bf16)
    return dot(order, stored_ref[0, round_index, 0], 1, 0)


def first_dispatch(grad, route_expert, route_slot, gates, capacity, senders, pieces):
    tokens, width = grad.shape
    rows = senders * capacity

    def body(grad_ref, expert_ref, slot_ref, gate_ref, table_ref, *out_refs):
        target = target_of(expert_ref[0, 0], slot_ref[0, 0], capacity)
        sent = dispatch_rows(grad_ref[...], gate_ref[0, 0], target, rows)
        split_rows(sent, out_refs, rows // pieces)
        later = target_of(expert_ref[0, 1], slot_ref[0, 1], capacity).astype(f32)
        lane = lax.broadcasted_iota(jnp.int32, table_ref.shape, 1)
        table_ref[...] = jnp.where(lane == 0, later, gate_ref[0, 1])

    table, *sent = on_chip(
        body,
        [jax.ShapeDtypeStruct((tokens, 2), f32)]
        + [jax.ShapeDtypeStruct((rows // pieces, width), bf16)] * pieces,
        (grad, route_expert, route_slot, gates),
        moved=3 * tokens * width * 2,
    )
    return table, sent


def hidden_blocks(saved_pre, senders, capacity, hidden_width, replicas):
    rows = senders * capacity
    aligned = (hidden_width // replicas) % 16 == 0
    block = hidden_width // replicas

    def body(stored_ref, *refs):
        *out_refs, held = refs
        for round_index in range(ROUNDS):
            stored = stored_rows(stored_ref, round_index, senders, capacity)
            gate_pre, up_value = stored[:, :hidden_width], stored[:, hidden_width:]
            hidden = (gate_pre * up_value) / (1.0 + jnp.exp(-gate_pre))
            held[:, round_index * rows : (round_index + 1) * rows] = hidden.T.astype(bf16)
        if not aligned:
            out_refs[0][...] = held[...]
            return
        mine = lax.axis_index("edp")
        for step, ref in enumerate(out_refs):
            start = pl.multiple_of((mine ^ step) * block, 16)
            ref[...] = held[pl.ds(start, block), :]

    shapes = (
        [jax.ShapeDtypeStruct((block, ROUNDS * rows), bf16)] * replicas
        if aligned
        else [jax.ShapeDtypeStruct((hidden_width, ROUNDS * rows), bf16)]
    )
    spec = pl.BlockSpec(memory_space=pltpu.VMEM)
    out = pl.pallas_call(
        body,
        out_shape=shapes,
        in_specs=[spec],
        out_specs=[spec] * len(shapes),
        scratch_shapes=[pltpu.VMEM((hidden_width, ROUNDS * rows), bf16)],
        compiler_params=pltpu.CompilerParams(vmem_limit_bytes=VMEM_LIMIT),
        cost_estimate=pl.CostEstimate(flops=0, bytes_accessed=2**20, transcendentals=0),
    )(saved_pre)
    if aligned:
        return out
    mine = lax.axis_index("edp")
    return [
        lax.dynamic_slice_in_dim(out[0], (mine ^ step) * block, block, 0)
        for step in range(replicas)
    ]


def expert_rows(pieces_in, saved_pre, w_gate_up, w_down, round_index, senders, capacity):
    rows = senders * capacity
    hidden_width, width = w_down.shape
    pieces = len(pieces_in)

    def body(stored_ref, up_ref, down_ref, *refs):
        in_refs, out_refs = refs[:pieces], refs[pieces:]
        routed = join_rows(in_refs)
        hidden_grad = dot(routed, down_ref[...], 1, 1)
        stored = stored_rows(stored_ref, round_index, senders, capacity)
        gate_pre, up_value = stored[:, :hidden_width], stored[:, hidden_width:]
        gate = 1.0 / (1.0 + jnp.exp(-gate_pre))
        act_grad = jnp.concatenate(
            [
                hidden_grad * up_value * gate * (1.0 + gate_pre * (1.0 - gate)),
                hidden_grad * gate_pre * gate,
            ],
            axis=1,
        ).astype(bf16)
        split_rows(dot(act_grad, up_ref[...], 1, 1), out_refs, rows // pieces)

    return on_chip(
        body,
        [jax.ShapeDtypeStruct((rows // pieces, width), bf16)] * pieces,
        (saved_pre, w_gate_up, w_down, *pieces_in),
        flops=6 * rows * hidden_width * width,
        moved=6 * hidden_width * width,
    )


def norm_backward(grad_out, branch, saved, gain):
    normed_in = saved.astype(f32)
    inverse = lax.rsqrt(jnp.mean(normed_in * normed_in, axis=1, keepdims=True) + NORM_EPS)
    scaled_in = normed_in * inverse
    norm_grad = branch * gain
    result = grad_out.astype(f32) + inverse * (
        norm_grad - scaled_in * jnp.mean(norm_grad * scaled_in, axis=1, keepdims=True)
    )
    return result.astype(bf16)


def first_combine(
    returned, grad, tail, saved_input, gain, route_expert, route_slot, table, capacity, senders
):
    tokens, width = grad.shape
    rows = senders * capacity
    pieces = len(returned)

    def body(grad_ref, tail_ref, saved_ref, gain_ref, expert_ref, slot_ref, table_ref, *refs):
        in_refs, (result_ref, *out_refs) = refs[:pieces], refs[pieces:]
        target = target_of(expert_ref[0, 0], slot_ref[0, 0], capacity)
        branch = dot(one_hot(target, rows), join_rows(in_refs), 1, 0)
        result = norm_backward(grad_ref[...], branch, saved_ref[0, 0], gain_ref[...])
        result_ref[...] = result
        first = lax.axis_index("pipe") == 0
        passed = jnp.where(first, tail_ref[...].astype(f32), result.astype(f32))
        later = table_ref[:, 0:1].astype(jnp.int32)
        split_rows(
            dispatch_rows(passed, table_ref[:, 1:2], later, rows), out_refs, rows // pieces
        )

    result, *sent = on_chip(
        body,
        [jax.ShapeDtypeStruct((tokens, width), bf16)]
        + [jax.ShapeDtypeStruct((rows // pieces, width), bf16)] * pieces,
        (grad, tail, saved_input, gain, route_expert, route_slot, table, *returned),
        moved=8 * tokens * width * 2,
    )
    return result, sent


def second_combine(
    returned, first_out, passed, tail, saved_input, gain, route_expert, route_slot, capacity, senders
):
    tokens, width = first_out.shape
    rows = senders * capacity
    pieces = len(returned)

    def body(first_ref, passed_ref, tail_ref, saved_ref, gain_ref, expert_ref, slot_ref, *refs):
        in_refs, (out_ref,) = refs[:pieces], refs[pieces:]
        out_ref[0, 0] = first_ref[...]
        target = target_of(expert_ref[0, 1], slot_ref[0, 1], capacity)
        branch = dot(one_hot(target, rows), join_rows(in_refs), 1, 0)
        last = lax.axis_index("pipe") == lax.axis_size("pipe") - 1
        grad = jnp.where(last, tail_ref[...].astype(f32), passed_ref[...].astype(f32))
        out_ref[0, 1] = norm_backward(grad, branch, saved_ref[0, 1], gain_ref[...])

    return on_chip(
        body,
        [jax.ShapeDtypeStruct((1, ROUNDS, tokens, width), bf16)],
        (first_out, passed, tail, saved_input, gain, route_expert, route_slot, *returned),
        moved=8 * tokens * width * 2,
    )[0]


def weight_grad(hidden, first_rows, second_rows, scale):
    replicas = len(hidden)
    block = hidden[0].shape[0]
    rows, width = first_rows[0].shape

    def body(*refs):
        hidden_refs = refs[:replicas]
        first_refs = refs[replicas : 2 * replicas]
        second_refs = refs[2 * replicas : 3 * replicas]
        out_ref = refs[-1]
        left = jnp.concatenate([ref[...] for ref in hidden_refs], axis=1)
        right = jnp.concatenate(
            [ref[...] for pair in zip(first_refs, second_refs) for ref in pair], axis=0
        )
        out_ref[0, 0] = dot(left, right, 1, 0) / scale

    return on_chip(
        body,
        [jax.ShapeDtypeStruct((1, 1, block, width), f32)],
        (*hidden, *first_rows, *second_rows),
        flops=4 * replicas * rows * block * width,
        moved=4 * block * width + 4 * replicas * rows * width,
    )[0]


def steps_over(axis, values):
    count = lax.axis_size(axis)
    return [values[0]] + [
        lax.ppermute(values[step], axis, [(source, source ^ step) for source in range(count)])
        for step in range(1, count)
    ]


def behind(values):
    sections, count = lax.axis_size("pipe"), lax.axis_size("expert")
    return [
        lax.ppermute(
            value,
            ("pipe", "expert"),
            [
                (section * count + source, (section - 1) % sections * count + (source ^ step))
                for section in range(sections)
                for source in range(count)
            ],
        )
        for step, value in enumerate(values)
    ]


def local(
    head_grads,
    tail_grad,
    saved_input,
    norm_gain,
    route_expert,
    route_slot,
    gates,
    saved_pre,
    w_gate_up,
    w_down,
):
    senders = lax.axis_size("expert")
    replicas = lax.axis_size("edp")
    sections = lax.axis_size("pipe")
    rows = saved_pre.shape[3]
    capacity = rows // senders
    width = w_down.shape[3]
    hidden_width = w_down.shape[2]
    pieces = senders if capacity % 16 == 0 else 1
    grad = head_grads[0]
    up, down = w_gate_up[0, 0], w_down[0, 0]

    def apart(parts):
        if pieces == senders:
            return parts
        return [parts[0][k * capacity : (k + 1) * capacity] for k in range(senders)]

    def together(parts):
        return parts if pieces == senders else [jnp.concatenate(parts, axis=0)]

    def whole(parts):
        return parts[0] if len(parts) == 1 else jnp.concatenate(parts, axis=0)

    def over_experts(parts):
        return together(steps_over("expert", apart(parts)))

    hidden = hidden_blocks(saved_pre, senders, capacity, hidden_width, replicas)
    hidden = steps_over("edp", hidden)

    table, sent = first_dispatch(
        grad, route_expert, route_slot, gates, capacity, senders, pieces
    )
    table = lax.ppermute(
        table, "pipe", [(source, (source + 1) % sections) for source in range(sections)]
    )
    arrived = over_experts(sent)
    first_rows = steps_over("edp", [whole(arrived)] * replicas)
    returned = over_experts(
        expert_rows(arrived, saved_pre, up, down, 0, senders, capacity)
    )
    first_out, sent = first_combine(
        returned,
        grad,
        tail_grad,
        saved_input,
        norm_gain,
        route_expert,
        route_slot,
        table,
        capacity,
        senders,
    )
    arrived = together(behind(apart(sent)))
    passed = lax.ppermute(
        first_out, "pipe", [(source, (source - 1) % sections) for source in range(sections)]
    )
    second_rows = steps_over("edp", [whole(arrived)] * replicas)
    returned = over_experts(
        expert_rows(arrived, saved_pre, up, down, 1, senders, capacity)
    )
    input_out = second_combine(
        returned,
        first_out,
        passed,
        tail_grad,
        saved_input,
        norm_gain,
        route_expert,
        route_slot,
        capacity,
        senders,
    )
    grad_shard = weight_grad(hidden, first_rows, second_rows, float(replicas * ROUNDS))
    return (input_out, grad_shard)


def solution(mesh):
    return jax.shard_map(
        local,
        mesh=mesh,
        in_specs=(
            P("pipe", ("expert", "edp"), None),
            P(("expert", "edp"), None),
            P("pipe", None, ("expert", "edp"), None),
            P("pipe", None),
            P("pipe", None, ("expert", "edp"), None),
            P("pipe", None, ("expert", "edp"), None),
            P("pipe", None, ("expert", "edp"), None),
            P("pipe", None, "expert", "edp", None),
            P("pipe", "expert", None, None),
            P("pipe", "expert", None, None),
        ),
        out_specs=(P("pipe", None, ("expert", "edp"), None), P("pipe", "expert", "edp", None)),
        check_vma=False,
    )
```

```python
import jax
import jax.numpy as jnp
from jax import lax
from jax.experimental import pallas as pl
from jax.experimental.pallas import tpu as pltpu
from jax.sharding import PartitionSpec as P

ROUNDS = 2
NORM_EPS = 1e-06
VMEM_LIMIT = 24 * 2**20

bf16 = jnp.bfloat16
f32 = jnp.float32


def on_chip(body, outs, args, fetched=(), after=(), scratch=(), flops=0, moved=0):
    whole = pl.BlockSpec(memory_space=pltpu.VMEM)
    there = pl.BlockSpec(memory_space=pltpu.HBM)
    anywhere = pl.BlockSpec(memory_space=pl.ANY)
    first, last = len(fetched), len(fetched) + len(after)

    def run(*refs):
        body(*refs[:first], *refs[last:])

    return pl.pallas_call(
        run,
        out_shape=outs,
        in_specs=[there] * first + [anywhere] * len(after) + [whole] * len(args),
        out_specs=jax.tree.map(lambda _: whole, outs),
        scratch_shapes=scratch,
        compiler_params=pltpu.CompilerParams(vmem_limit_bytes=VMEM_LIMIT),
        cost_estimate=pl.CostEstimate(flops=flops, bytes_accessed=moved, transcendentals=0),
    )(*[pltpu.with_memory_space_constraint(value, pltpu.HBM) for value in fetched], *after, *args)


def fetch(copies, sems):
    started = [
        pltpu.make_async_copy(source, target, sems.at[index])
        for index, (source, target) in enumerate(copies)
    ]
    for copy in started:
        copy.start()
    return started


def dot(left, right, left_dim, right_dim):
    return lax.dot_general(
        left, right, (((left_dim,), (right_dim,)), ((), ())), preferred_element_type=f32
    )


def split_rows(value, refs, rows):
    for index, ref in enumerate(refs):
        ref[...] = value[index * rows : (index + 1) * rows].astype(ref.dtype)


def join_rows(refs):
    if len(refs) == 1:
        return refs[0][...]
    return jnp.concatenate([ref[...] for ref in refs], axis=0)


def column(row):
    count = row.shape[1]
    down = lax.broadcasted_iota(jnp.int32, (count, count), 0)
    along = lax.broadcasted_iota(jnp.int32, (count, count), 1)
    return jnp.sum(jnp.where(down == along, row, jnp.zeros_like(row)), axis=1, keepdims=True)


def one_hot(target, rows):
    down = lax.broadcasted_iota(jnp.int32, (rows, target.shape[1]), 0)
    return jnp.where(target == down, 1.0, 0.0).astype(bf16)


def target_of(expert, slot, capacity):
    mine = lax.axis_index("expert")
    return (expert ^ mine) * capacity + slot


def dispatch_rows(grad, gate, target, rows):
    scaled = (grad.astype(f32) * column(gate)).astype(bf16)
    return dot(one_hot(target, rows), scaled, 1, 0)


def stored_rows(stored_ref, round_index, senders, capacity):
    mine = lax.axis_index("expert")
    if capacity % 16 == 0:
        return jnp.concatenate(
            [
                stored_ref[
                    0,
                    round_index,
                    0,
                    pl.ds(pl.multiple_of((mine ^ step) * capacity, 16), capacity),
                    :,
                ]
                for step in range(senders)
            ],
            axis=0,
        ).astype(f32)
    rows = senders * capacity
    row = lax.broadcasted_iota(jnp.int32, (rows, rows), 0)
    column = lax.broadcasted_iota(jnp.int32, (rows, rows), 1)
    moved = ((row // capacity) ^ mine) * capacity + row % capacity
    order = jnp.where(moved == column, 1.0, 0.0).astype(bf16)
    return dot(order, stored_ref[0, round_index, 0], 1, 0)


def rides_along(block, rows, width, replicas):
    return (
        replicas == 4
        and block % 16 == 0
        and ROUNDS * rows == 128
        and block // 16 * 128 <= width
    )


def join(arrived, hidden, after):
    rows, width = sum(part.shape[0] for part in arrived), arrived[0].shape[1]

    def body(*refs):
        hidden_refs, refs = refs[:3], refs[3:]
        in_refs, (rows_ref, near_ref, far_ref) = refs[: len(arrived)], refs[len(arrived) :]
        value = join_rows(in_refs)
        rows_ref[...] = value
        near_ref[0:rows, :] = value
        near_ref[rows : rows + 16, :] = hidden_refs[0][...]
        far_ref[0:16, :] = hidden_refs[1][...]
        far_ref[16 : rows + 16, :] = value
        far_ref[rows + 16 : rows + 32, :] = hidden_refs[2][...]

    return on_chip(
        body,
        [
            jax.ShapeDtypeStruct((rows, width), bf16),
            jax.ShapeDtypeStruct((rows + 16, width), bf16),
            jax.ShapeDtypeStruct((rows + 32, width), bf16),
        ],
        (*hidden[1:], *arrived),
        after=after,
        moved=8 * rows * width,
    )


def unpack(ref, start, block, columns):
    return jnp.concatenate(
        [
            ref[start : start + 16, 128 * part : 128 * (part + 1)][:, columns]
            for part in range(block // 16)
        ],
        axis=0,
    )


def first_dispatch(
    grad, route_expert, route_slot, gates, saved_pre, capacity, senders, pieces, replicas
):
    tokens, width = grad.shape
    rows = senders * capacity
    hidden_width = saved_pre.shape[4] // 2
    block = hidden_width // replicas
    packed = rides_along(block, rows, width, replicas)
    hidden_shapes = (
        [jax.ShapeDtypeStruct((16, width), bf16)] * replicas
        if packed
        else [jax.ShapeDtypeStruct((hidden_width, ROUNDS * rows), bf16)]
    )

    def body(grad_in, expert_in, slot_in, gate_in, stored_in, *refs):
        table_ref, stored_ref, *refs = refs
        sent_refs, refs = refs[:pieces], refs[pieces:]
        hidden_refs, refs = refs[: len(hidden_shapes)], refs[len(hidden_shapes) :]
        grad_ref, expert_ref, slot_ref, gate_ref, held, sems = refs
        copies = fetch(
            (
                (expert_in, expert_ref),
                (slot_in, slot_ref),
                (gate_in, gate_ref),
                (grad_in, grad_ref),
                (stored_in, stored_ref),
            ),
            sems,
        )
        for copy in copies[:4]:
            copy.wait()
        target = target_of(expert_ref[0, 0], slot_ref[0, 0], capacity)
        sent = dispatch_rows(grad_ref[...], gate_ref[0, 0], target, rows)
        split_rows(sent, sent_refs, rows // pieces)
        later = target_of(expert_ref[0, 1], slot_ref[0, 1], capacity).astype(f32)
        table_ref[0:1, :] = later
        table_ref[1:2, :] = gate_ref[0, 1]
        copies[4].wait()
        for round_index in range(ROUNDS):
            stored = stored_rows(stored_ref, round_index, senders, capacity)
            gate_pre, up_value = stored[:, :hidden_width], stored[:, hidden_width:]
            hidden = (gate_pre * up_value) / (1.0 + jnp.exp(-gate_pre))
            held[:, round_index * rows : (round_index + 1) * rows] = hidden.T.astype(bf16)
        if not packed:
            hidden_refs[0][...] = held[...]
            return
        mine = lax.axis_index("edp")
        for step, ref in enumerate(hidden_refs):
            ref[...] = jnp.zeros_like(ref)
            for part in range(block // 16):
                start = pl.multiple_of((mine ^ step) * block + 16 * part, 16)
                ref[:, 128 * part : 128 * (part + 1)] = held[pl.ds(start, 16), :]

    table, stored, *made = on_chip(
        body,
        [jax.ShapeDtypeStruct((2, tokens), f32), jax.ShapeDtypeStruct(saved_pre.shape, bf16)]
        + [jax.ShapeDtypeStruct((rows // pieces, width), bf16)] * pieces
        + hidden_shapes,
        (),
        fetched=(grad, route_expert, route_slot, gates, saved_pre),
        scratch=[
            pltpu.VMEM(grad.shape, bf16),
            pltpu.VMEM(route_expert.shape, jnp.int32),
            pltpu.VMEM(route_slot.shape, jnp.int32),
            pltpu.VMEM(gates.shape, f32),
            pltpu.VMEM((hidden_width, ROUNDS * rows), bf16),
            pltpu.SemaphoreType.DMA((5,)),
        ],
        moved=3 * tokens * width * 2,
    )
    sent, hidden = made[:pieces], made[pieces:]
    if not packed:
        mine = lax.axis_index("edp")
        hidden = [
            lax.dynamic_slice_in_dim(hidden[0], (mine ^ step) * block, block, 0)
            for step in range(replicas)
        ]
    return table, sent, stored, hidden


def prepare(w_gate_up, w_down, after):
    def body(up_in, down_in, up_ref, down_ref, sems):
        for copy in fetch(((down_in, down_ref), (up_in, up_ref)), sems):
            copy.wait()

    return on_chip(
        body,
        [
            jax.ShapeDtypeStruct(w_gate_up.shape, bf16),
            jax.ShapeDtypeStruct(w_down.shape, bf16),
        ],
        (),
        fetched=(w_gate_up, w_down),
        after=after,
        scratch=[pltpu.SemaphoreType.DMA((2,))],
        moved=2 * (w_gate_up.size + w_down.size),
    )


def expert_rows(
    pieces_in, saved_pre, w_gate_up, w_down, round_index, senders, capacity, pieces, after=()
):
    rows = senders * capacity
    hidden_width, width = w_down.shape

    def body(stored_ref, up_ref, down_ref, *refs):
        in_refs, out_refs = refs[: len(pieces_in)], refs[len(pieces_in) :]
        routed = join_rows(in_refs)
        hidden_grad = dot(routed, down_ref[...], 1, 1)
        stored = stored_rows(stored_ref, round_index, senders, capacity)
        gate_pre, up_value = stored[:, :hidden_width], stored[:, hidden_width:]
        gate = 1.0 / (1.0 + jnp.exp(-gate_pre))
        act_grad = jnp.concatenate(
            [
                hidden_grad * up_value * gate * (1.0 + gate_pre * (1.0 - gate)),
                hidden_grad * gate_pre * gate,
            ],
            axis=1,
        ).astype(bf16)
        split_rows(dot(act_grad, up_ref[...], 1, 1), out_refs, rows // pieces)

    return on_chip(
        body,
        [jax.ShapeDtypeStruct((rows // pieces, width), bf16)] * pieces,
        (saved_pre, w_gate_up, w_down, *pieces_in),
        after=after,
        flops=6 * rows * hidden_width * width,
        moved=6 * hidden_width * width,
    )


def norm_backward(grad_out, branch, saved, gain):
    normed_in = saved.astype(f32)
    inverse = lax.rsqrt(jnp.mean(normed_in * normed_in, axis=1, keepdims=True) + NORM_EPS)
    scaled_in = normed_in * inverse
    norm_grad = branch * gain
    result = grad_out.astype(f32) + inverse * (
        norm_grad - scaled_in * jnp.mean(norm_grad * scaled_in, axis=1, keepdims=True)
    )
    return result.astype(bf16)


def first_combine(
    returned, grad, tail, saved_input, gain, route_expert, route_slot, table, capacity, senders, after=()
):
    tokens, width = grad.shape
    rows = senders * capacity
    pieces = len(returned)

    def body(grad_ref, tail_ref, saved_ref, gain_ref, expert_ref, slot_ref, table_ref, *refs):
        in_refs, (result_ref, *out_refs) = refs[:pieces], refs[pieces:]
        target = target_of(expert_ref[0, 0], slot_ref[0, 0], capacity)
        branch = dot(one_hot(target, rows), join_rows(in_refs), 0, 0)
        result = norm_backward(grad_ref[...], branch, saved_ref[0, 0], gain_ref[...])
        result_ref[...] = result
        first = lax.axis_index("pipe") == 0
        passed = jnp.where(first, tail_ref[...].astype(f32), result.astype(f32))
        later = table_ref[0:1, :].astype(jnp.int32)
        split_rows(
            dispatch_rows(passed, table_ref[1:2, :], later, rows), out_refs, rows // pieces
        )

    result, *sent = on_chip(
        body,
        [jax.ShapeDtypeStruct((tokens, width), bf16)]
        + [jax.ShapeDtypeStruct((rows // pieces, width), bf16)] * pieces,
        (grad, tail, saved_input, gain, route_expert, route_slot, table, *returned),
        after=after,
        moved=8 * tokens * width * 2,
    )
    return result, sent


def second_combine(
    returned, first_out, passed, tail, saved_input, gain, route_expert, route_slot, capacity, senders, after=()
):
    tokens, width = first_out.shape
    rows = senders * capacity
    pieces = len(returned)

    def body(first_ref, passed_ref, tail_ref, saved_ref, gain_ref, expert_ref, slot_ref, *refs):
        in_refs, (out_ref,) = refs[:pieces], refs[pieces:]
        out_ref[0, 0] = first_ref[...]
        target = target_of(expert_ref[0, 1], slot_ref[0, 1], capacity)
        branch = dot(one_hot(target, rows), join_rows(in_refs), 0, 0)
        last = lax.axis_index("pipe") == lax.axis_size("pipe") - 1
        grad = jnp.where(last, tail_ref[...].astype(f32), passed_ref[...].astype(f32))
        out_ref[0, 1] = norm_backward(grad, branch, saved_ref[0, 1], gain_ref[...])

    return on_chip(
        body,
        [jax.ShapeDtypeStruct((1, ROUNDS, tokens, width), bf16)],
        (first_out, passed, tail, saved_input, gain, route_expert, route_slot, *returned),
        after=after,
        moved=8 * tokens * width * 2,
    )[0]


def weight_grad(left, right, round_index, rows, block, scale=None, earlier=None):
    lefts, rights = [array for array, _ in left], [array for array, _ in right]
    width = rights[0].shape[1]
    arrays = []
    for array in lefts + rights:
        if not any(array is other for other in arrays):
            arrays.append(array)
    place = [next(i for i, other in enumerate(arrays) if other is a) for a in lefts + rights]

    def body(*refs):
        columns = slice(round_index * rows, (round_index + 1) * rows)
        left_value = jnp.concatenate(
            [
                refs[where][:, columns]
                if start is None
                else unpack(refs[where], start, block, columns)
                for where, (_, start) in zip(place, left)
            ],
            axis=1,
        )
        right_value = jnp.concatenate(
            [
                refs[where][start : start + rows, :]
                for where, (_, start) in zip(place[len(left) :], right)
            ],
            axis=0,
        )
        total = dot(left_value, right_value, 1, 0)
        if earlier is not None:
            total = (refs[len(arrays)][0, 0] + total) / scale
        refs[-1][0, 0] = total

    return on_chip(
        body,
        [jax.ShapeDtypeStruct((1, 1, block, width), f32)],
        tuple(arrays) + (() if earlier is None else (earlier,)),
        flops=2 * len(left) * rows * block * width,
        moved=8 * block * width,
    )[0]


def steps_over(axis, values):
    count = lax.axis_size(axis)
    return [values[0]] + [
        lax.ppermute(values[step], axis, [(source, source ^ step) for source in range(count)])
        for step in range(1, count)
    ]


def step_over(value, step):
    count = lax.axis_size("edp")
    return lax.ppermute(value, "edp", [(source, source ^ step) for source in range(count)])


def behind(values):
    sections, count = lax.axis_size("pipe"), lax.axis_size("expert")
    return [
        lax.ppermute(
            value,
            ("pipe", "expert"),
            [
                (section * count + source, (section - 1) % sections * count + (source ^ step))
                for section in range(sections)
                for source in range(count)
            ],
        )
        for step, value in enumerate(values)
    ]


def local(
    head_grads,
    tail_grad,
    saved_input,
    norm_gain,
    route_expert,
    route_slot,
    gates,
    saved_pre,
    w_gate_up,
    w_down,
):
    senders = lax.axis_size("expert")
    replicas = lax.axis_size("edp")
    sections = lax.axis_size("pipe")
    rows = saved_pre.shape[3]
    capacity = rows // senders
    width = w_down.shape[3]
    hidden_width = w_down.shape[2]
    pieces = senders if capacity % 16 == 0 else 1
    grad = head_grads[0]
    up, down = w_gate_up[0, 0], w_down[0, 0]

    def apart(parts):
        if pieces == senders:
            return parts
        return [parts[0][k * capacity : (k + 1) * capacity] for k in range(senders)]

    def together(parts):
        return parts if pieces == senders else [jnp.concatenate(parts, axis=0)]

    def whole(parts):
        return parts[0] if len(parts) == 1 else jnp.concatenate(parts, axis=0)

    def over_experts(parts):
        return together(steps_over("expert", apart(parts)))

    route_expert, route_slot, gates = (
        jnp.transpose(value, (0, 1, 3, 2)) for value in (route_expert, route_slot, gates)
    )
    table, sent, stored, hidden = first_dispatch(
        grad,
        route_expert,
        route_slot,
        gates,
        saved_pre,
        capacity,
        senders,
        pieces,
        replicas,
    )
    up, down = prepare(up, down, after=(table,))
    table = lax.ppermute(
        table, "pipe", [(source, (source + 1) % sections) for source in range(sections)]
    )
    arrived = over_experts(sent)
    block = hidden_width // replicas
    if rides_along(block, rows, width, replicas):
        joined, near_load, far_load = join(arrived, hidden, after=(up, down, table))
        far = step_over(far_load, 2)
        near = step_over(near_load, 1)
        last = step_over(far[16:], 1)
        left = [(hidden[0], 0), (near, rows), (far, 0), (last, rows)]
        right = [(joined, 0), (near, 0), (far, 16), (last, 0)]
        arrived = [joined]
        early, late = (near,), (last,)
    else:
        first_rows = [whole(arrived)] * replicas
        left = [(value, None) for value in steps_over("edp", hidden)]
        right = [(value, 0) for value in steps_over("edp", first_rows)]
        early = late = ()
    returned = over_experts(
        expert_rows(arrived, stored, up, down, 0, senders, capacity, pieces)
    )
    first_out, sent = first_combine(
        returned,
        grad,
        tail_grad,
        saved_input,
        norm_gain,
        route_expert,
        route_slot,
        table,
        capacity,
        senders,
        after=early,
    )
    arrived = together(behind(apart(sent)))
    passed = lax.ppermute(
        first_out, "pipe", [(source, (source - 1) % sections) for source in range(sections)]
    )
    joined = whole(arrived)
    if replicas == 4:
        far = step_over(joined, 2)
        near = step_over(joined, 1)
        second_right = [joined, near, far, step_over(far, 1)]
    else:
        second_right = steps_over("edp", [joined] * replicas)
    first_share = weight_grad(left, right, 0, rows, block)
    returned = over_experts(
        expert_rows(
            arrived, stored, up, down, 1, senders, capacity, pieces, after=late
        )
    )
    input_out = second_combine(
        returned,
        first_out,
        passed,
        tail_grad,
        saved_input,
        norm_gain,
        route_expert,
        route_slot,
        capacity,
        senders,
        after=(first_share,),
    )
    grad_shard = weight_grad(
        left,
        [(value, 0) for value in second_right],
        1,
        rows,
        block,
        scale=float(replicas * ROUNDS),
        earlier=first_share,
    )
    return (input_out, grad_shard)


def solution(mesh):
    return jax.shard_map(
        local,
        mesh=mesh,
        in_specs=(
            P("pipe", ("expert", "edp"), None),
            P(("expert", "edp"), None),
            P("pipe", None, ("expert", "edp"), None),
            P("pipe", None),
            P("pipe", None, ("expert", "edp"), None),
            P("pipe", None, ("expert", "edp"), None),
            P("pipe", None, ("expert", "edp"), None),
            P("pipe", None, "expert", "edp", None),
            P("pipe", "expert", None, None),
            P("pipe", "expert", None, None),
        ),
        out_specs=(P("pipe", None, ("expert", "edp"), None), P("pipe", "expert", "edp", None)),
        check_vma=False,
    )
```

```python
import jax
import jax.numpy as jnp
from jax import lax
from jax.experimental import pallas as pl
from jax.experimental.pallas import tpu as pltpu
from jax.sharding import PartitionSpec as P

ROUNDS = 2
NORM_EPS = 1e-06
VMEM_LIMIT = 24 * 2**20

bf16 = jnp.bfloat16
f32 = jnp.float32


def on_chip(body, outs, args, fetched=(), after=(), scratch=(), flops=0, moved=0):
    whole = pl.BlockSpec(memory_space=pltpu.VMEM)
    there = pl.BlockSpec(memory_space=pltpu.HBM)
    anywhere = pl.BlockSpec(memory_space=pl.ANY)
    first, last = len(fetched), len(fetched) + len(after)

    def run(*refs):
        body(*refs[:first], *refs[last:])

    return pl.pallas_call(
        run,
        out_shape=outs,
        in_specs=[there] * first + [anywhere] * len(after) + [whole] * len(args),
        out_specs=jax.tree.map(lambda _: whole, outs),
        scratch_shapes=scratch,
        compiler_params=pltpu.CompilerParams(vmem_limit_bytes=VMEM_LIMIT),
        cost_estimate=pl.CostEstimate(flops=flops, bytes_accessed=moved, transcendentals=0),
    )(*[pltpu.with_memory_space_constraint(value, pltpu.HBM) for value in fetched], *after, *args)


def fetch(copies, sems):
    started = [
        pltpu.make_async_copy(source, target, sems.at[index])
        for index, (source, target) in enumerate(copies)
    ]
    for copy in started:
        copy.start()
    return started


def dot(left, right, left_dim, right_dim):
    return lax.dot_general(
        left, right, (((left_dim,), (right_dim,)), ((), ())), preferred_element_type=f32
    )


def even(senders, capacity):
    return senders == 4 and capacity % 16 == 0


def sent_shapes(senders, capacity, width, pairs=False):
    if not even(senders, capacity):
        return [jax.ShapeDtypeStruct((senders * capacity, width), bf16)]
    if pairs:
        return [jax.ShapeDtypeStruct((2 * capacity, width), bf16)] * 2
    return [jax.ShapeDtypeStruct((capacity, width), bf16)] * senders


def spread(value, refs, capacity):
    count = len(refs)
    if count == 1:
        refs[0][...] = value.astype(bf16)
        return
    for first, ref in enumerate(refs):
        for place in range(4 // count):
            start = (first + count * place) * capacity
            ref[place * capacity : (place + 1) * capacity] = value[
                start : start + capacity
            ].astype(bf16)


def collect(refs, capacity):
    if len(refs) == 1:
        return refs[0][...]
    if len(refs) == 3:
        return jnp.concatenate(
            [refs[0][0:capacity], refs[1][0:capacity], refs[2][...]], axis=0
        )
    return jnp.concatenate([ref[...] for ref in refs], axis=0)


def pair_up(stays, came, capacity, places, after=()):
    def body(stays_ref, came_ref, *refs):
        for place, ref in zip(places, refs):
            part = slice(place * capacity, (place + 1) * capacity)
            ref[0:capacity] = stays_ref[part]
            ref[capacity : 2 * capacity] = came_ref[part]

    return on_chip(
        body,
        [jax.ShapeDtypeStruct(stays.shape, bf16)] * len(places),
        (stays, came),
        after=after,
        moved=8 * capacity * stays.shape[1],
    )


def column(row):
    count = row.shape[1]
    down = lax.broadcasted_iota(jnp.int32, (count, count), 0)
    along = lax.broadcasted_iota(jnp.int32, (count, count), 1)
    return jnp.sum(jnp.where(down == along, row, jnp.zeros_like(row)), axis=1, keepdims=True)


def one_hot(target, rows):
    down = lax.broadcasted_iota(jnp.int32, (rows, target.shape[1]), 0)
    return jnp.where(target == down, 1.0, 0.0).astype(bf16)


def target_of(expert, slot, capacity):
    mine = lax.axis_index("expert")
    return (expert ^ mine) * capacity + slot


def dispatch_rows(grad, gate, target, rows):
    scaled = (grad.astype(f32) * column(gate)).astype(bf16)
    return dot(one_hot(target, rows), scaled, 1, 0)


def stored_rows(stored_ref, round_index, senders, capacity):
    mine = lax.axis_index("expert")
    if capacity % 16 == 0:
        return jnp.concatenate(
            [
                stored_ref[
                    0,
                    round_index,
                    0,
                    pl.ds(pl.multiple_of((mine ^ step) * capacity, 16), capacity),
                    :,
                ]
                for step in range(senders)
            ],
            axis=0,
        ).astype(f32)
    rows = senders * capacity
    row = lax.broadcasted_iota(jnp.int32, (rows, rows), 0)
    column = lax.broadcasted_iota(jnp.int32, (rows, rows), 1)
    moved = ((row // capacity) ^ mine) * capacity + row % capacity
    order = jnp.where(moved == column, 1.0, 0.0).astype(bf16)
    return dot(order, stored_ref[0, round_index, 0], 1, 0)


def rides_along(block, rows, width, replicas):
    return (
        replicas == 4
        and block % 16 == 0
        and ROUNDS * rows == 128
        and block // 16 * 128 <= width
    )


def join(arrived, hidden, capacity, rows, after=()):
    width = arrived[0].shape[1]

    def body(*refs):
        hidden_refs, refs = refs[: len(hidden)], refs[len(hidden) :]
        in_refs, (rows_ref, *load_refs) = refs[: len(arrived)], refs[len(arrived) :]
        value = collect(in_refs, capacity)
        rows_ref[...] = value
        for hidden_ref, load_ref in zip(hidden_refs, load_refs):
            load_ref[0:rows, :] = value
            load_ref[rows : rows + 16, :] = hidden_ref[...]

    joined, *loads = on_chip(
        body,
        [jax.ShapeDtypeStruct((rows, width), bf16)]
        + [jax.ShapeDtypeStruct((rows + 16, width), bf16)] * len(hidden),
        (*hidden, *arrived),
        after=after,
        moved=8 * rows * width,
    )
    return joined, loads


def first_rows_of(value, rows, after):
    def body(value_ref, out_ref):
        out_ref[...] = value_ref[0:rows, :]

    return on_chip(
        body,
        [jax.ShapeDtypeStruct((rows, value.shape[1]), value.dtype)],
        (value,),
        after=after,
        moved=4 * rows * value.shape[1],
    )[0]


def unpack(ref, start, block, columns):
    return jnp.concatenate(
        [
            ref[start : start + 16, 128 * part : 128 * (part + 1)][:, columns]
            for part in range(block // 16)
        ],
        axis=0,
    )


def first_dispatch(
    grad, route_expert, route_slot, gates, saved_pre, w_down, capacity, senders, replicas
):
    tokens, width = grad.shape
    rows = senders * capacity
    hidden_width = saved_pre.shape[4] // 2
    block = hidden_width // replicas
    packed = rides_along(block, rows, width, replicas)
    sent_to = sent_shapes(senders, capacity, width)
    hidden_shapes = (
        [jax.ShapeDtypeStruct((16, width), bf16)] * 4
        if packed
        else [jax.ShapeDtypeStruct((hidden_width, ROUNDS * rows), bf16)]
    )

    def body(grad_in, expert_in, slot_in, gate_in, stored_in, down_in, *refs):
        table_ref, stored_ref, down_ref, *refs = refs
        sent_refs, refs = refs[: len(sent_to)], refs[len(sent_to) :]
        hidden_refs, refs = refs[: len(hidden_shapes)], refs[len(hidden_shapes) :]
        grad_ref, expert_ref, slot_ref, gate_ref, held, sems = refs
        copies = fetch(
            (
                (expert_in, expert_ref),
                (slot_in, slot_ref),
                (gate_in, gate_ref),
                (grad_in, grad_ref),
                (stored_in, stored_ref),
                (down_in, down_ref),
            ),
            sems,
        )
        for copy in copies[:4]:
            copy.wait()
        target = target_of(expert_ref[0, 0], slot_ref[0, 0], capacity)
        sent = dispatch_rows(grad_ref[...], gate_ref[0, 0], target, rows)
        spread(sent, sent_refs, capacity)
        later = target_of(expert_ref[0, 1], slot_ref[0, 1], capacity).astype(f32)
        table_ref[0:1, :] = later
        table_ref[1:2, :] = gate_ref[0, 1]
        copies[4].wait()
        for round_index in range(ROUNDS):
            stored = stored_rows(stored_ref, round_index, senders, capacity)
            gate_pre, up_value = stored[:, :hidden_width], stored[:, hidden_width:]
            hidden = (gate_pre * up_value) / (1.0 + jnp.exp(-gate_pre))
            held[:, round_index * rows : (round_index + 1) * rows] = hidden.T.astype(bf16)
        if not packed:
            hidden_refs[0][...] = held[...]
            copies[5].wait()
            return
        mine = lax.axis_index("edp")
        for step, ref in enumerate(hidden_refs):
            ref[...] = jnp.zeros_like(ref)
            for part in range(block // 16):
                start = pl.multiple_of((mine ^ step) * block + 16 * part, 16)
                ref[:, 128 * part : 128 * (part + 1)] = held[pl.ds(start, 16), :]
        copies[5].wait()

    table, stored, down, *made = on_chip(
        body,
        [
            jax.ShapeDtypeStruct((2, tokens), f32),
            jax.ShapeDtypeStruct(saved_pre.shape, bf16),
            jax.ShapeDtypeStruct(w_down.shape, bf16),
        ]
        + sent_to
        + hidden_shapes,
        (),
        fetched=(grad, route_expert, route_slot, gates, saved_pre, w_down),
        scratch=[
            pltpu.VMEM(grad.shape, bf16),
            pltpu.VMEM(route_expert.shape, jnp.int32),
            pltpu.VMEM(route_slot.shape, jnp.int32),
            pltpu.VMEM(gates.shape, f32),
            pltpu.VMEM((hidden_width, ROUNDS * rows), bf16),
            pltpu.SemaphoreType.DMA((6,)),
        ],
        moved=3 * tokens * width * 2,
    )
    sent, hidden = made[: len(sent_to)], made[len(sent_to) :]
    if not packed:
        mine = lax.axis_index("edp")
        hidden = [
            lax.dynamic_slice_in_dim(hidden[0], (mine ^ step) * block, block, 0)
            for step in range(replicas)
        ]
    return table, sent, stored, down, hidden


def bring(value, after):
    def body(value_in, value_ref, sems):
        for copy in fetch(((value_in, value_ref),), sems):
            copy.wait()

    return on_chip(
        body,
        [jax.ShapeDtypeStruct(value.shape, value.dtype)],
        (),
        fetched=(value,),
        after=after,
        scratch=[pltpu.SemaphoreType.DMA((1,))],
        moved=2 * value.size,
    )[0]


def expert_rows(
    pieces_in, saved_pre, w_gate_up, w_down, round_index, senders, capacity, pairs=False, after=()
):
    rows = senders * capacity
    hidden_width, width = w_down.shape

    def body(stored_ref, up_ref, down_ref, *refs):
        in_refs, out_refs = refs[: len(pieces_in)], refs[len(pieces_in) :]
        routed = collect(in_refs, capacity)
        hidden_grad = dot(routed, down_ref[...], 1, 1)
        stored = stored_rows(stored_ref, round_index, senders, capacity)
        gate_pre, up_value = stored[:, :hidden_width], stored[:, hidden_width:]
        gate = 1.0 / (1.0 + jnp.exp(-gate_pre))
        act_grad = jnp.concatenate(
            [
                hidden_grad * up_value * gate * (1.0 + gate_pre * (1.0 - gate)),
                hidden_grad * gate_pre * gate,
            ],
            axis=1,
        ).astype(bf16)
        spread(dot(act_grad, up_ref[...], 1, 1), out_refs, capacity)

    return on_chip(
        body,
        sent_shapes(senders, capacity, width, pairs),
        (saved_pre, w_gate_up, w_down, *pieces_in),
        after=after,
        flops=6 * rows * hidden_width * width,
        moved=6 * hidden_width * width,
    )


def norm_backward(grad_out, branch, saved, gain):
    normed_in = saved.astype(f32)
    inverse = lax.rsqrt(jnp.mean(normed_in * normed_in, axis=1, keepdims=True) + NORM_EPS)
    scaled_in = normed_in * inverse
    norm_grad = branch * gain
    result = grad_out.astype(f32) + inverse * (
        norm_grad - scaled_in * jnp.mean(norm_grad * scaled_in, axis=1, keepdims=True)
    )
    return result.astype(bf16)


def first_combine(
    returned, grad, tail, saved_input, gain, route_expert, route_slot, table, capacity, senders, after=()
):
    tokens, width = grad.shape
    rows = senders * capacity
    pieces = len(returned)

    def body(grad_ref, tail_ref, saved_ref, gain_ref, expert_ref, slot_ref, table_ref, *refs):
        in_refs, (result_ref, *out_refs) = refs[:pieces], refs[pieces:]
        target = target_of(expert_ref[0, 0], slot_ref[0, 0], capacity)
        branch = dot(one_hot(target, rows), collect(in_refs, capacity), 0, 0)
        result = norm_backward(grad_ref[...], branch, saved_ref[0, 0], gain_ref[...])
        result_ref[...] = result
        first = lax.axis_index("pipe") == 0
        passed = jnp.where(first, tail_ref[...].astype(f32), result.astype(f32))
        later = table_ref[0:1, :].astype(jnp.int32)
        spread(dispatch_rows(passed, table_ref[1:2, :], later, rows), out_refs, capacity)

    result, *sent = on_chip(
        body,
        [jax.ShapeDtypeStruct((tokens, width), bf16)]
        + sent_shapes(senders, capacity, width),
        (grad, tail, saved_input, gain, route_expert, route_slot, table, *returned),
        after=after,
        moved=8 * tokens * width * 2,
    )
    return result, sent


def second_combine(
    returned, first_out, passed, tail, saved_input, gain, route_expert, route_slot, capacity, senders, after=()
):
    tokens, width = first_out.shape
    rows = senders * capacity
    pieces = len(returned)

    def body(first_ref, passed_ref, tail_ref, saved_ref, gain_ref, expert_ref, slot_ref, *refs):
        in_refs, (out_ref, token_ref) = refs[:pieces], refs[pieces:]
        token_ref[...] = jnp.zeros_like(token_ref)
        out_ref[0, 0] = first_ref[...]
        target = target_of(expert_ref[0, 1], slot_ref[0, 1], capacity)
        branch = dot(one_hot(target, rows), collect(in_refs, capacity), 0, 0)
        last = lax.axis_index("pipe") == lax.axis_size("pipe") - 1
        grad = jnp.where(last, tail_ref[...].astype(f32), passed_ref[...].astype(f32))
        out_ref[0, 1] = norm_backward(grad, branch, saved_ref[0, 1], gain_ref[...])

    return on_chip(
        body,
        [
            jax.ShapeDtypeStruct((1, ROUNDS, tokens, width), bf16),
            jax.ShapeDtypeStruct((8, 128), f32),
        ],
        (first_out, passed, tail, saved_input, gain, route_expert, route_slot, *returned),
        after=after,
        moved=8 * tokens * width * 2,
    )


def weight_grad(terms, rows, block, scale=None, earlier=None, after=()):
    width = terms[0][3].shape[1]
    arrays = []
    for term in terms:
        for array in (term[0], term[3]):
            if not any(array is other for other in arrays):
                arrays.append(array)

    def place(array):
        return next(index for index, other in enumerate(arrays) if other is array)

    places = [(place(left), start, number, place(right)) for left, start, number, right in terms]

    def body(*refs):
        lefts, rights = [], []
        for left, start, number, right in places:
            columns = slice(number * rows, (number + 1) * rows)
            if start is None:
                lefts.append(refs[left][:, columns])
            else:
                lefts.append(unpack(refs[left], start, block, columns))
            rights.append(refs[right][0:rows, :])
        total = dot(jnp.concatenate(lefts, axis=1), jnp.concatenate(rights, axis=0), 1, 0)
        if earlier is not None:
            total = (refs[len(arrays)][0, 0] + total) / scale
        refs[-1][0, 0] = total

    return on_chip(
        body,
        [jax.ShapeDtypeStruct((1, 1, block, width), f32)],
        tuple(arrays) + (() if earlier is None else (earlier,)),
        after=after,
        flops=2 * len(terms) * rows * block * width,
        moved=8 * block * width,
    )[0]


def at_distance(value, axis, step):
    count = lax.axis_size(axis)
    return lax.ppermute(value, axis, [(source, source ^ step) for source in range(count)])


def steps_over(axis, values):
    return [values[0]] + [
        at_distance(value, axis, step) for step, value in enumerate(values) if step
    ]


def behind(values):
    sections, count = lax.axis_size("pipe"), lax.axis_size("expert")
    return [
        lax.ppermute(
            value,
            ("pipe", "expert"),
            [
                (section * count + source, (section - 1) % sections * count + (source ^ step))
                for section in range(sections)
                for source in range(count)
            ],
        )
        for step, value in values
    ]


def local(
    head_grads,
    tail_grad,
    saved_input,
    norm_gain,
    route_expert,
    route_slot,
    gates,
    saved_pre,
    w_gate_up,
    w_down,
):
    senders = lax.axis_size("expert")
    replicas = lax.axis_size("edp")
    sections = lax.axis_size("pipe")
    rows = saved_pre.shape[3]
    capacity = rows // senders
    width = w_down.shape[3]
    hidden_width = w_down.shape[2]
    grad = head_grads[0]
    up, down = w_gate_up[0, 0], w_down[0, 0]

    def apart(parts):
        if len(parts) == senders:
            return parts
        return [parts[0][k * capacity : (k + 1) * capacity] for k in range(senders)]

    def together(parts, like):
        return parts if len(like) == senders else [jnp.concatenate(parts, axis=0)]

    def over_experts(parts, after=()):
        if even(senders, capacity) and len(parts) == 2:
            stays, turns = parts
            came = at_distance(turns, "expert", 1)
            (load,) = pair_up(stays, came, capacity, (1,), after)
            return [stays, came, at_distance(load, "expert", 2)]
        return together(steps_over("expert", apart(parts)), parts)

    def back(parts):
        return together(behind(list(enumerate(apart(parts)))), parts)

    route_expert, route_slot, gates = (
        jnp.transpose(value, (0, 1, 3, 2)) for value in (route_expert, route_slot, gates)
    )
    table, sent, stored, down, hidden = first_dispatch(
        grad,
        route_expert,
        route_slot,
        gates,
        saved_pre,
        down,
        capacity,
        senders,
        replicas,
    )
    up = bring(up, after=(table,))
    table = lax.ppermute(
        table, "pipe", [(source, (source + 1) % sections) for source in range(sections)]
    )
    arrived = over_experts(sent)
    block = hidden_width // replicas
    if rides_along(block, rows, width, replicas):
        joined, (near_load,) = join(
            arrived, hidden[1:2], capacity, rows, after=(up, table)
        )
        far = at_distance(joined, "edp", 2)
        near = at_distance(near_load, "edp", 1)
        arrived = [joined]
        early = (near, far)
        arrived = [joined]
    else:
        left = steps_over("edp", hidden)
        right = steps_over("edp", arrived * replicas)
        early = ()
    sent = expert_rows(
        arrived, stored, up, down, 0, senders, capacity
    )
    returned = over_experts(sent)
    first_out, sent = first_combine(
        returned,
        grad,
        tail_grad,
        saved_input,
        norm_gain,
        route_expert,
        route_slot,
        table,
        capacity,
        senders,
        after=early,
    )
    if early:
        last = at_distance(first_rows_of(far, rows, (sent[0],)), "edp", 1)
    arrived = back(sent)
    passed = lax.ppermute(
        first_out, "pipe", [(source, (source - 1) % sections) for source in range(sections)]
    )
    if rides_along(block, rows, width, replicas):
        again, _ = join(arrived, (), capacity, rows)
        second = at_distance(again, "edp", 2)
        first = at_distance(again, "edp", 1)
        third = at_distance(second, "edp", 1)
        units = [at_distance(hidden[step], "edp", step) for step in (2, 3)]
        arrived, late, tail = [again], (last,), (first,)
        now = [(hidden[0], 0, 0, joined), (near, rows, 0, near), (units[0], 0, 0, far)]
        then = [
            (hidden[0], 0, 1, again),
            (near, rows, 1, first),
            (units[0], 0, 1, second),
            (units[1], 0, 1, third),
            (units[1], 0, 0, last),
        ]
    else:
        late = tail = ()
        again = steps_over("edp", arrived * replicas)
        now = [(units, None, 0, value) for units, value in zip(left, right)]
        then = [(units, None, 1, value) for units, value in zip(left, again)]
    first_share = weight_grad(now, rows, block)
    returned = over_experts(
        expert_rows(
            arrived, stored, up, down, 1, senders, capacity, pairs=True, after=late
        ),
        after=tail,
    )
    input_out, done = second_combine(
        returned,
        first_out,
        passed,
        tail_grad,
        saved_input,
        norm_gain,
        route_expert,
        route_slot,
        capacity,
        senders,
        after=(first_share,),
    )
    grad_shard = weight_grad(
        then, rows, block, scale=float(replicas * ROUNDS), earlier=first_share, after=(done,)
    )
    return (input_out, grad_shard)


def solution(mesh):
    return jax.shard_map(
        local,
        mesh=mesh,
        in_specs=(
            P("pipe", ("expert", "edp"), None),
            P(("expert", "edp"), None),
            P("pipe", None, ("expert", "edp"), None),
            P("pipe", None),
            P("pipe", None, ("expert", "edp"), None),
            P("pipe", None, ("expert", "edp"), None),
            P("pipe", None, ("expert", "edp"), None),
            P("pipe", None, "expert", "edp", None),
            P("pipe", "expert", None, None),
            P("pipe", "expert", None, None),
        ),
        out_specs=(P("pipe", None, ("expert", "edp"), None), P("pipe", "expert", "edp", None)),
        check_vma=False,
    )
```

```python
import jax
import jax.numpy as jnp
from jax import lax
from jax.experimental import pallas as pl
from jax.experimental.pallas import tpu as pltpu
from jax.sharding import PartitionSpec as P

ROUNDS = 2
NORM_EPS = 1e-06
VMEM_LIMIT = 24 * 2**20

bf16 = jnp.bfloat16
f32 = jnp.float32


def on_chip(
    body, outs, args, fetched=(), after=(), scratch=(), flops=0, moved=0, sends=False
):
    whole = pl.BlockSpec(memory_space=pltpu.VMEM)
    there = pl.BlockSpec(memory_space=pltpu.HBM)
    anywhere = pl.BlockSpec(memory_space=pl.ANY)
    first, last = len(fetched), len(fetched) + len(after)

    def run(*refs):
        body(*refs[:first], *refs[last:])

    return pl.pallas_call(
        run,
        out_shape=outs,
        in_specs=[there] * first + [anywhere] * len(after) + [whole] * len(args),
        out_specs=jax.tree.map(lambda _: anywhere if sends else whole, outs),
        scratch_shapes=scratch,
        compiler_params=pltpu.CompilerParams(vmem_limit_bytes=VMEM_LIMIT),
        cost_estimate=pl.CostEstimate(flops=flops, bytes_accessed=moved, transcendentals=0),
    )(*[pltpu.with_memory_space_constraint(value, pltpu.HBM) for value in fetched], *after, *args)


def fetch(copies, sems):
    started = [
        pltpu.make_async_copy(source, target, sems.at[index])
        for index, (source, target) in enumerate(copies)
    ]
    for copy in started:
        copy.start()
    return started


def dot(left, right, left_dim, right_dim):
    return lax.dot_general(
        left, right, (((left_dim,), (right_dim,)), ((), ())), preferred_element_type=f32
    )


def even(senders, capacity):
    return senders == 4 and capacity % 16 == 0


def sent_shapes(senders, capacity, width, pairs=False):
    if not even(senders, capacity):
        return [jax.ShapeDtypeStruct((senders * capacity, width), bf16)]
    if pairs:
        return [jax.ShapeDtypeStruct((2 * capacity, width), bf16)] * 2
    return [jax.ShapeDtypeStruct((capacity, width), bf16)] * senders


def spread(value, refs, capacity):
    count = len(refs)
    if count == 1:
        refs[0][...] = value.astype(bf16)
        return
    for first, ref in enumerate(refs):
        for place in range(4 // count):
            start = (first + count * place) * capacity
            ref[place * capacity : (place + 1) * capacity] = value[
                start : start + capacity
            ].astype(bf16)


def collect(refs, capacity):
    if len(refs) == 1:
        return refs[0][...]
    if len(refs) == 3:
        return jnp.concatenate(
            [refs[0][0:capacity], refs[1][0:capacity], refs[2][...]], axis=0
        )
    return jnp.concatenate([ref[...] for ref in refs], axis=0)


def pair_up(stays, came, capacity, places, after=()):
    def body(stays_ref, came_ref, *refs):
        for place, ref in zip(places, refs):
            part = slice(place * capacity, (place + 1) * capacity)
            ref[0:capacity] = stays_ref[part]
            ref[capacity : 2 * capacity] = came_ref[part]

    return on_chip(
        body,
        [jax.ShapeDtypeStruct(stays.shape, bf16)] * len(places),
        (stays, came),
        after=after,
        moved=8 * capacity * stays.shape[1],
    )


def column(row):
    count = row.shape[1]
    down = lax.broadcasted_iota(jnp.int32, (count, count), 0)
    along = lax.broadcasted_iota(jnp.int32, (count, count), 1)
    return jnp.sum(jnp.where(down == along, row, jnp.zeros_like(row)), axis=1, keepdims=True)


def one_hot(target, rows):
    down = lax.broadcasted_iota(jnp.int32, (rows, target.shape[1]), 0)
    return jnp.where(target == down, 1.0, 0.0).astype(bf16)


def target_of(expert, slot, capacity):
    mine = lax.axis_index("expert")
    return (expert ^ mine) * capacity + slot


def dispatch_rows(grad, gate, target, rows):
    scaled = (grad.astype(f32) * column(gate)).astype(bf16)
    return dot(one_hot(target, rows), scaled, 1, 0)


def stored_rows(stored_ref, round_index, senders, capacity):
    mine = lax.axis_index("expert")
    if capacity % 16 == 0:
        return jnp.concatenate(
            [
                stored_ref[
                    0,
                    round_index,
                    0,
                    pl.ds(pl.multiple_of((mine ^ step) * capacity, 16), capacity),
                    :,
                ]
                for step in range(senders)
            ],
            axis=0,
        ).astype(f32)
    rows = senders * capacity
    row = lax.broadcasted_iota(jnp.int32, (rows, rows), 0)
    column = lax.broadcasted_iota(jnp.int32, (rows, rows), 1)
    moved = ((row // capacity) ^ mine) * capacity + row % capacity
    order = jnp.where(moved == column, 1.0, 0.0).astype(bf16)
    return dot(order, stored_ref[0, round_index, 0], 1, 0)


def rides_along(block, rows, width, replicas):
    return (
        replicas == 4
        and block % 16 == 0
        and ROUNDS * rows == 128
        and block // 16 * 128 <= width
    )


def join(arrived, hidden, capacity, rows, after=()):
    width = arrived[0].shape[1]

    def body(*refs):
        hidden_refs, refs = refs[: len(hidden)], refs[len(hidden) :]
        in_refs, (rows_ref, *load_refs) = refs[: len(arrived)], refs[len(arrived) :]
        value = collect(in_refs, capacity)
        rows_ref[...] = value
        for hidden_ref, load_ref in zip(hidden_refs, load_refs):
            load_ref[0:rows, :] = value
            load_ref[rows : rows + 16, :] = hidden_ref[...]

    joined, *loads = on_chip(
        body,
        [jax.ShapeDtypeStruct((rows, width), bf16)]
        + [jax.ShapeDtypeStruct((rows + 16, width), bf16)] * len(hidden),
        (*hidden, *arrived),
        after=after,
        moved=8 * rows * width,
    )
    return joined, loads


def first_rows_of(value, rows, after):
    def body(value_ref, out_ref):
        out_ref[...] = value_ref[0:rows, :]

    return on_chip(
        body,
        [jax.ShapeDtypeStruct((rows, value.shape[1]), value.dtype)],
        (value,),
        after=after,
        moved=4 * rows * value.shape[1],
    )[0]


def unpack(ref, start, block, columns):
    return jnp.concatenate(
        [
            ref[start : start + 16, 128 * part : 128 * (part + 1)][:, columns]
            for part in range(block // 16)
        ],
        axis=0,
    )


def first_dispatch(
    grad, route_expert, route_slot, gates, saved_pre, w_down, capacity, senders, replicas
):
    tokens, width = grad.shape
    rows = senders * capacity
    hidden_width = saved_pre.shape[4] // 2
    block = hidden_width // replicas
    packed = rides_along(block, rows, width, replicas)
    sent_to = sent_shapes(senders, capacity, width)
    hidden_shapes = (
        [jax.ShapeDtypeStruct((16, width), bf16)] * 4
        if packed
        else [jax.ShapeDtypeStruct((hidden_width, ROUNDS * rows), bf16)]
    )

    def body(grad_in, expert_in, slot_in, gate_in, stored_in, down_in, *refs):
        table_ref, stored_ref, down_ref, *refs = refs
        sent_refs, refs = refs[: len(sent_to)], refs[len(sent_to) :]
        hidden_refs, refs = refs[: len(hidden_shapes)], refs[len(hidden_shapes) :]
        grad_ref, expert_ref, slot_ref, gate_ref, held, sems = refs
        copies = fetch(
            (
                (expert_in, expert_ref),
                (slot_in, slot_ref),
                (gate_in, gate_ref),
                (grad_in, grad_ref),
                (stored_in, stored_ref),
                (down_in, down_ref),
            ),
            sems,
        )
        for copy in copies[:4]:
            copy.wait()
        target = target_of(expert_ref[0, 0], slot_ref[0, 0], capacity)
        sent = dispatch_rows(grad_ref[...], gate_ref[0, 0], target, rows)
        spread(sent, sent_refs, capacity)
        later = target_of(expert_ref[0, 1], slot_ref[0, 1], capacity).astype(f32)
        table_ref[0:1, :] = later
        table_ref[1:2, :] = gate_ref[0, 1]
        copies[4].wait()
        for round_index in range(ROUNDS):
            stored = stored_rows(stored_ref, round_index, senders, capacity)
            gate_pre, up_value = stored[:, :hidden_width], stored[:, hidden_width:]
            hidden = (gate_pre * up_value) / (1.0 + jnp.exp(-gate_pre))
            held[:, round_index * rows : (round_index + 1) * rows] = hidden.T.astype(bf16)
        if not packed:
            hidden_refs[0][...] = held[...]
            copies[5].wait()
            return
        mine = lax.axis_index("edp")
        for step, ref in enumerate(hidden_refs):
            ref[...] = jnp.zeros_like(ref)
            for part in range(block // 16):
                start = pl.multiple_of((mine ^ step) * block + 16 * part, 16)
                ref[:, 128 * part : 128 * (part + 1)] = held[pl.ds(start, 16), :]
        copies[5].wait()

    table, stored, down, *made = on_chip(
        body,
        [
            jax.ShapeDtypeStruct((2, tokens), f32),
            jax.ShapeDtypeStruct(saved_pre.shape, bf16),
            jax.ShapeDtypeStruct(w_down.shape, bf16),
        ]
        + sent_to
        + hidden_shapes,
        (),
        fetched=(grad, route_expert, route_slot, gates, saved_pre, w_down),
        scratch=[
            pltpu.VMEM(grad.shape, bf16),
            pltpu.VMEM(route_expert.shape, jnp.int32),
            pltpu.VMEM(route_slot.shape, jnp.int32),
            pltpu.VMEM(gates.shape, f32),
            pltpu.VMEM((hidden_width, ROUNDS * rows), bf16),
            pltpu.SemaphoreType.DMA((6,)),
        ],
        moved=3 * tokens * width * 2,
    )
    sent, hidden = made[: len(sent_to)], made[len(sent_to) :]
    if not packed:
        mine = lax.axis_index("edp")
        hidden = [
            lax.dynamic_slice_in_dim(hidden[0], (mine ^ step) * block, block, 0)
            for step in range(replicas)
        ]
    return table, sent, stored, down, hidden


def bring(value, after):
    def body(value_in, value_ref, sems):
        for copy in fetch(((value_in, value_ref),), sems):
            copy.wait()

    return on_chip(
        body,
        [jax.ShapeDtypeStruct(value.shape, value.dtype)],
        (),
        fetched=(value,),
        after=after,
        scratch=[pltpu.SemaphoreType.DMA((1,))],
        moved=2 * value.size,
    )[0]


def expert_rows(
    pieces_in, saved_pre, w_gate_up, w_down, round_index, senders, capacity, pairs=False, after=()
):
    rows = senders * capacity
    hidden_width, width = w_down.shape

    def body(stored_ref, up_ref, down_ref, *refs):
        in_refs, out_refs = refs[: len(pieces_in)], refs[len(pieces_in) :]
        routed = collect(in_refs, capacity)
        hidden_grad = dot(routed, down_ref[...], 1, 1)
        stored = stored_rows(stored_ref, round_index, senders, capacity)
        gate_pre, up_value = stored[:, :hidden_width], stored[:, hidden_width:]
        gate = 1.0 / (1.0 + jnp.exp(-gate_pre))
        act_grad = jnp.concatenate(
            [
                hidden_grad * up_value * gate * (1.0 + gate_pre * (1.0 - gate)),
                hidden_grad * gate_pre * gate,
            ],
            axis=1,
        ).astype(bf16)
        spread(dot(act_grad, up_ref[...], 1, 1), out_refs, capacity)

    return on_chip(
        body,
        sent_shapes(senders, capacity, width, pairs),
        (saved_pre, w_gate_up, w_down, *pieces_in),
        after=after,
        flops=6 * rows * hidden_width * width,
        moved=6 * hidden_width * width,
    )


def norm_backward(grad_out, branch, saved, gain):
    normed_in = saved.astype(f32)
    inverse = lax.rsqrt(jnp.mean(normed_in * normed_in, axis=1, keepdims=True) + NORM_EPS)
    scaled_in = normed_in * inverse
    norm_grad = branch * gain
    result = grad_out.astype(f32) + inverse * (
        norm_grad - scaled_in * jnp.mean(norm_grad * scaled_in, axis=1, keepdims=True)
    )
    return result.astype(bf16)


def first_combine(
    returned, grad, tail, saved_input, gain, route_expert, route_slot, table, capacity, senders, after=()
):
    tokens, width = grad.shape
    rows = senders * capacity
    pieces = len(returned)

    def body(grad_ref, tail_ref, saved_ref, gain_ref, expert_ref, slot_ref, table_ref, *refs):
        in_refs, (result_ref, *out_refs) = refs[:pieces], refs[pieces:]
        target = target_of(expert_ref[0, 0], slot_ref[0, 0], capacity)
        branch = dot(one_hot(target, rows), collect(in_refs, capacity), 0, 0)
        result = norm_backward(grad_ref[...], branch, saved_ref[0, 0], gain_ref[...])
        result_ref[...] = result
        first = lax.axis_index("pipe") == 0
        passed = jnp.where(first, tail_ref[...].astype(f32), result.astype(f32))
        later = table_ref[0:1, :].astype(jnp.int32)
        spread(dispatch_rows(passed, table_ref[1:2, :], later, rows), out_refs, capacity)

    result, *sent = on_chip(
        body,
        [jax.ShapeDtypeStruct((tokens, width), bf16)]
        + sent_shapes(senders, capacity, width),
        (grad, tail, saved_input, gain, route_expert, route_slot, table, *returned),
        after=after,
        moved=8 * tokens * width * 2,
    )
    return result, sent


def second_combine(
    returned, first_out, passed, tail, saved_input, gain, route_expert, route_slot, capacity, senders, after=()
):
    tokens, width = first_out.shape
    rows = senders * capacity
    pieces = len(returned)

    def body(first_ref, passed_ref, tail_ref, saved_ref, gain_ref, expert_ref, slot_ref, *refs):
        in_refs, (out_ref, token_ref) = refs[:pieces], refs[pieces:]
        token_ref[...] = jnp.zeros_like(token_ref)
        out_ref[0, 0] = first_ref[...]
        target = target_of(expert_ref[0, 1], slot_ref[0, 1], capacity)
        branch = dot(one_hot(target, rows), collect(in_refs, capacity), 0, 0)
        last = lax.axis_index("pipe") == lax.axis_size("pipe") - 1
        grad = jnp.where(last, tail_ref[...].astype(f32), passed_ref[...].astype(f32))
        out_ref[0, 1] = norm_backward(grad, branch, saved_ref[0, 1], gain_ref[...])

    return on_chip(
        body,
        [
            jax.ShapeDtypeStruct((1, ROUNDS, tokens, width), bf16),
            jax.ShapeDtypeStruct((8, 128), f32),
        ],
        (first_out, passed, tail, saved_input, gain, route_expert, route_slot, *returned),
        after=after,
        moved=8 * tokens * width * 2,
    )


def weight_grad(terms, rows, block, scale=None, earlier=None, after=()):
    width = terms[0][3].shape[1]
    arrays = []
    for term in terms:
        for array in (term[0], term[3]):
            if not any(array is other for other in arrays):
                arrays.append(array)

    def place(array):
        return next(index for index, other in enumerate(arrays) if other is array)

    sends = earlier is not None and block % 8 == 0 and width % 256 == 0
    parts = width // 256
    part = 256
    places = [(place(left), start, number, place(right)) for left, start, number, right in terms]

    def body(*refs):
        lefts, rights = [], []
        for left, start, number, right in places:
            columns = slice(number * rows, (number + 1) * rows)
            if start is None:
                lefts.append(refs[left][:, columns])
            else:
                lefts.append(unpack(refs[left], start, block, columns))
            rights.append(refs[right][0:rows, :])
        left_value = jnp.concatenate(lefts, axis=1)
        right_value = jnp.concatenate(rights, axis=0)
        if not sends:
            total = dot(left_value, right_value, 1, 0)
            if earlier is not None:
                total = (refs[len(arrays)][0, 0] + total) / scale
            refs[-1][0, 0] = total
            return
        out_ref, held, sems = refs[-3:]
        copies = []
        for index in range(parts):
            columns = slice(index * part, (index + 1) * part)
            total = dot(left_value, right_value[:, columns], 1, 0)
            held[:, columns] = (refs[len(arrays)][0, 0, :, columns] + total) / scale
            copies.append(
                pltpu.make_async_copy(
                    held.at[:, pl.ds(index * part, part)],
                    out_ref.at[0, 0, :, pl.ds(index * part, part)],
                    sems.at[index],
                )
            )
            copies[-1].start()
        for copy in copies:
            copy.wait()

    return on_chip(
        body,
        [jax.ShapeDtypeStruct((1, 1, block, width), f32)],
        tuple(arrays) + (() if earlier is None else (earlier,)),
        after=after,
        scratch=[pltpu.VMEM((block, width), f32), pltpu.SemaphoreType.DMA((parts,))]
        if sends
        else (),
        sends=sends,
        flops=2 * len(terms) * rows * block * width,
        moved=8 * block * width,
    )[0]


def at_distance(value, axis, step):
    count = lax.axis_size(axis)
    return lax.ppermute(value, axis, [(source, source ^ step) for source in range(count)])


def steps_over(axis, values):
    return [values[0]] + [
        at_distance(value, axis, step) for step, value in enumerate(values) if step
    ]


def behind(values):
    sections, count = lax.axis_size("pipe"), lax.axis_size("expert")
    return [
        lax.ppermute(
            value,
            ("pipe", "expert"),
            [
                (section * count + source, (section - 1) % sections * count + (source ^ step))
                for section in range(sections)
                for source in range(count)
            ],
        )
        for step, value in values
    ]


def local(
    head_grads,
    tail_grad,
    saved_input,
    norm_gain,
    route_expert,
    route_slot,
    gates,
    saved_pre,
    w_gate_up,
    w_down,
):
    senders = lax.axis_size("expert")
    replicas = lax.axis_size("edp")
    sections = lax.axis_size("pipe")
    rows = saved_pre.shape[3]
    capacity = rows // senders
    width = w_down.shape[3]
    hidden_width = w_down.shape[2]
    grad = head_grads[0]
    up, down = w_gate_up[0, 0], w_down[0, 0]

    def apart(parts):
        if len(parts) == senders:
            return parts
        return [parts[0][k * capacity : (k + 1) * capacity] for k in range(senders)]

    def together(parts, like):
        return parts if len(like) == senders else [jnp.concatenate(parts, axis=0)]

    def over_experts(parts, after=()):
        if even(senders, capacity) and len(parts) == 2:
            stays, turns = parts
            came = at_distance(turns, "expert", 1)
            (load,) = pair_up(stays, came, capacity, (1,), after)
            return [stays, came, at_distance(load, "expert", 2)]
        return together(steps_over("expert", apart(parts)), parts)

    def back(parts):
        return together(behind(list(enumerate(apart(parts)))), parts)

    route_expert, route_slot, gates = (
        jnp.transpose(value, (0, 1, 3, 2)) for value in (route_expert, route_slot, gates)
    )
    table, sent, stored, down, hidden = first_dispatch(
        grad,
        route_expert,
        route_slot,
        gates,
        saved_pre,
        down,
        capacity,
        senders,
        replicas,
    )
    up = bring(up, after=(table,))
    table = lax.ppermute(
        table, "pipe", [(source, (source + 1) % sections) for source in range(sections)]
    )
    arrived = over_experts(sent)
    block = hidden_width // replicas
    if rides_along(block, rows, width, replicas):
        joined, (near_load,) = join(
            arrived, hidden[1:2], capacity, rows, after=(up, table)
        )
        far = at_distance(joined, "edp", 2)
        near = at_distance(near_load, "edp", 1)
        arrived = [joined]
        early = (near, far)
        arrived = [joined]
    else:
        left = steps_over("edp", hidden)
        right = steps_over("edp", arrived * replicas)
        early = ()
    sent = expert_rows(
        arrived, stored, up, down, 0, senders, capacity
    )
    returned = over_experts(sent)
    first_out, sent = first_combine(
        returned,
        grad,
        tail_grad,
        saved_input,
        norm_gain,
        route_expert,
        route_slot,
        table,
        capacity,
        senders,
        after=early,
    )
    if early:
        last = at_distance(first_rows_of(far, rows, (sent[0],)), "edp", 1)
    arrived = back(sent)
    passed = lax.ppermute(
        first_out, "pipe", [(source, (source - 1) % sections) for source in range(sections)]
    )
    if rides_along(block, rows, width, replicas):
        again, _ = join(arrived, (), capacity, rows)
        second = at_distance(again, "edp", 2)
        first = at_distance(again, "edp", 1)
        third = at_distance(second, "edp", 1)
        units = [at_distance(hidden[step], "edp", step) for step in (2, 3)]
        arrived, late, tail = [again], (last,), (first,)
        now = [
            (hidden[0], 0, 0, joined),
            (near, rows, 0, near),
            (units[0], 0, 0, far),
            (hidden[0], 0, 1, again),
            (near, rows, 1, first),
            (units[0], 0, 1, second),
        ]
        then = [(units[1], 0, 0, last), (units[1], 0, 1, third)]
    else:
        late = tail = ()
        again = steps_over("edp", arrived * replicas)
        now = [(units, None, 0, value) for units, value in zip(left, right)]
        then = [(units, None, 1, value) for units, value in zip(left, again)]
    first_share = weight_grad(now, rows, block)
    returned = over_experts(
        expert_rows(
            arrived, stored, up, down, 1, senders, capacity, pairs=True, after=late
        ),
        after=tail,
    )
    input_out, done = second_combine(
        returned,
        first_out,
        passed,
        tail_grad,
        saved_input,
        norm_gain,
        route_expert,
        route_slot,
        capacity,
        senders,
        after=(first_share,),
    )
    grad_shard = weight_grad(
        then, rows, block, scale=float(replicas * ROUNDS), earlier=first_share, after=(done,)
    )
    return (input_out, grad_shard)


def solution(mesh):
    return jax.shard_map(
        local,
        mesh=mesh,
        in_specs=(
            P("pipe", ("expert", "edp"), None),
            P(("expert", "edp"), None),
            P("pipe", None, ("expert", "edp"), None),
            P("pipe", None),
            P("pipe", None, ("expert", "edp"), None),
            P("pipe", None, ("expert", "edp"), None),
            P("pipe", None, ("expert", "edp"), None),
            P("pipe", None, "expert", "edp", None),
            P("pipe", "expert", None, None),
            P("pipe", "expert", None, None),
        ),
        out_specs=(P("pipe", None, ("expert", "edp"), None), P("pipe", "expert", "edp", None)),
        check_vma=False,
    )
```

```python
import jax
import jax.numpy as jnp
from jax import lax
from jax.experimental import pallas as pl
from jax.experimental.pallas import tpu as pltpu
from jax.sharding import PartitionSpec as P

ROUNDS = 2
NORM_EPS = 1e-06
VMEM_LIMIT = 24 * 2**20

bf16 = jnp.bfloat16
f32 = jnp.float32


def on_chip(
    body, outs, args, fetched=(), after=(), scratch=(), flops=0, moved=0, sends=False
):
    whole = pl.BlockSpec(memory_space=pltpu.VMEM)
    there = pl.BlockSpec(memory_space=pltpu.HBM)
    anywhere = pl.BlockSpec(memory_space=pl.ANY)
    first, last = len(fetched), len(fetched) + len(after)

    def run(*refs):
        body(*refs[:first], *refs[last:])

    return pl.pallas_call(
        run,
        out_shape=outs,
        in_specs=[there] * first + [anywhere] * len(after) + [whole] * len(args),
        out_specs=jax.tree.map(lambda _: anywhere if sends else whole, outs),
        scratch_shapes=scratch,
        compiler_params=pltpu.CompilerParams(vmem_limit_bytes=VMEM_LIMIT),
        cost_estimate=pl.CostEstimate(flops=flops, bytes_accessed=moved, transcendentals=0),
    )(*[pltpu.with_memory_space_constraint(value, pltpu.HBM) for value in fetched], *after, *args)


def fetch(copies, sems):
    started = [
        pltpu.make_async_copy(source, target, sems.at[index])
        for index, (source, target) in enumerate(copies)
    ]
    for copy in started:
        copy.start()
    return started


def dot(left, right, left_dim, right_dim):
    return lax.dot_general(
        left, right, (((left_dim,), (right_dim,)), ((), ())), preferred_element_type=f32
    )


def even(senders, capacity):
    return senders == 4 and capacity % 16 == 0


def sent_shapes(senders, capacity, width, pairs=False):
    if not even(senders, capacity):
        return [jax.ShapeDtypeStruct((senders * capacity, width), bf16)]
    if pairs:
        return [jax.ShapeDtypeStruct((2 * capacity, width), bf16)] * 2
    return [jax.ShapeDtypeStruct((capacity, width), bf16)] * senders


def spread(value, refs, capacity):
    count = len(refs)
    if count == 1:
        refs[0][...] = value.astype(bf16)
        return
    for first, ref in enumerate(refs):
        for place in range(4 // count):
            start = (first + count * place) * capacity
            ref[place * capacity : (place + 1) * capacity] = value[
                start : start + capacity
            ].astype(bf16)


def collect(refs, capacity):
    if len(refs) == 1:
        return refs[0][...]
    if len(refs) == 3:
        return jnp.concatenate(
            [refs[0][0:capacity], refs[1][0:capacity], refs[2][...]], axis=0
        )
    return jnp.concatenate([ref[...] for ref in refs], axis=0)


def pair_up(stays, came, capacity, places, after=()):
    def body(stays_ref, came_ref, *refs):
        for place, ref in zip(places, refs):
            part = slice(place * capacity, (place + 1) * capacity)
            ref[0:capacity] = stays_ref[part]
            ref[capacity : 2 * capacity] = came_ref[part]

    return on_chip(
        body,
        [jax.ShapeDtypeStruct(stays.shape, bf16)] * len(places),
        (stays, came),
        after=after,
        moved=8 * capacity * stays.shape[1],
    )


def column(row):
    count = row.shape[1]
    down = lax.broadcasted_iota(jnp.int32, (count, count), 0)
    along = lax.broadcasted_iota(jnp.int32, (count, count), 1)
    return jnp.sum(jnp.where(down == along, row, jnp.zeros_like(row)), axis=1, keepdims=True)


def one_hot(target, rows):
    down = lax.broadcasted_iota(jnp.int32, (rows, target.shape[1]), 0)
    return jnp.where(target == down, 1.0, 0.0).astype(bf16)


def target_of(expert, slot, capacity):
    mine = lax.axis_index("expert")
    return (expert ^ mine) * capacity + slot


def dispatch_rows(grad, gate, target, rows):
    scaled = (grad.astype(f32) * column(gate)).astype(bf16)
    return dot(one_hot(target, rows), scaled, 1, 0)


def stored_rows(stored_ref, round_index, senders, capacity):
    mine = lax.axis_index("expert")
    if capacity % 16 == 0:
        return jnp.concatenate(
            [
                stored_ref[
                    0,
                    round_index,
                    0,
                    pl.ds(pl.multiple_of((mine ^ step) * capacity, 16), capacity),
                    :,
                ]
                for step in range(senders)
            ],
            axis=0,
        ).astype(f32)
    rows = senders * capacity
    row = lax.broadcasted_iota(jnp.int32, (rows, rows), 0)
    column = lax.broadcasted_iota(jnp.int32, (rows, rows), 1)
    moved = ((row // capacity) ^ mine) * capacity + row % capacity
    order = jnp.where(moved == column, 1.0, 0.0).astype(bf16)
    return dot(order, stored_ref[0, round_index, 0], 1, 0)


def rides_along(block, rows, width, replicas):
    return (
        replicas == 4
        and block % 16 == 0
        and ROUNDS * rows == 128
        and block // 16 * 128 <= width
    )


def join(arrived, hidden, capacity, rows, after=()):
    width = arrived[0].shape[1]

    def body(*refs):
        hidden_refs, refs = refs[: len(hidden)], refs[len(hidden) :]
        in_refs, (rows_ref, *load_refs) = refs[: len(arrived)], refs[len(arrived) :]
        value = collect(in_refs, capacity)
        rows_ref[...] = value
        for hidden_ref, load_ref in zip(hidden_refs, load_refs):
            load_ref[0:rows, :] = value
            load_ref[rows : rows + 16, :] = hidden_ref[...]

    joined, *loads = on_chip(
        body,
        [jax.ShapeDtypeStruct((rows, width), bf16)]
        + [jax.ShapeDtypeStruct((rows + 16, width), bf16)] * len(hidden),
        (*hidden, *arrived),
        after=after,
        moved=8 * rows * width,
    )
    return joined, loads


def first_rows_of(value, rows, after):
    def body(value_ref, out_ref):
        out_ref[...] = value_ref[0:rows, :]

    return on_chip(
        body,
        [jax.ShapeDtypeStruct((rows, value.shape[1]), value.dtype)],
        (value,),
        after=after,
        moved=4 * rows * value.shape[1],
    )[0]


def unpack(ref, start, block, columns):
    return jnp.concatenate(
        [
            ref[start : start + 16, 128 * part : 128 * (part + 1)][:, columns]
            for part in range(block // 16)
        ],
        axis=0,
    )


def first_dispatch(
    grad, route_expert, route_slot, gates, saved_pre, w_down, capacity, senders, replicas
):
    tokens, width = grad.shape
    rows = senders * capacity
    hidden_width = saved_pre.shape[4] // 2
    block = hidden_width // replicas
    packed = rides_along(block, rows, width, replicas)
    sent_to = sent_shapes(senders, capacity, width)
    hidden_shapes = (
        [jax.ShapeDtypeStruct((16, width), bf16)] * 4
        if packed
        else [jax.ShapeDtypeStruct((hidden_width, ROUNDS * rows), bf16)]
    )

    def body(grad_in, expert_in, slot_in, gate_in, stored_in, down_in, *refs):
        table_ref, stored_ref, down_ref, *refs = refs
        sent_refs, refs = refs[: len(sent_to)], refs[len(sent_to) :]
        hidden_refs, refs = refs[: len(hidden_shapes)], refs[len(hidden_shapes) :]
        grad_ref, expert_ref, slot_ref, gate_ref, held, sems = refs
        copies = fetch(
            (
                (expert_in, expert_ref),
                (slot_in, slot_ref),
                (gate_in, gate_ref),
                (grad_in, grad_ref),
                (stored_in, stored_ref),
                (down_in, down_ref),
            ),
            sems,
        )
        for copy in copies[:4]:
            copy.wait()
        target = target_of(expert_ref[0, 0], slot_ref[0, 0], capacity)
        sent = dispatch_rows(grad_ref[...], gate_ref[0, 0], target, rows)
        spread(sent, sent_refs, capacity)
        later = target_of(expert_ref[0, 1], slot_ref[0, 1], capacity).astype(f32)
        table_ref[0:1, :] = later
        table_ref[1:2, :] = gate_ref[0, 1]
        copies[4].wait()
        for round_index in range(ROUNDS):
            stored = stored_rows(stored_ref, round_index, senders, capacity)
            gate_pre, up_value = stored[:, :hidden_width], stored[:, hidden_width:]
            hidden = (gate_pre * up_value) / (1.0 + jnp.exp(-gate_pre))
            held[:, round_index * rows : (round_index + 1) * rows] = hidden.T.astype(bf16)
        if not packed:
            hidden_refs[0][...] = held[...]
            copies[5].wait()
            return
        mine = lax.axis_index("edp")
        for step, ref in enumerate(hidden_refs):
            ref[...] = jnp.zeros_like(ref)
            for part in range(block // 16):
                start = pl.multiple_of((mine ^ step) * block + 16 * part, 16)
                ref[:, 128 * part : 128 * (part + 1)] = held[pl.ds(start, 16), :]
        copies[5].wait()

    table, stored, down, *made = on_chip(
        body,
        [
            jax.ShapeDtypeStruct((2, tokens), f32),
            jax.ShapeDtypeStruct(saved_pre.shape, bf16),
            jax.ShapeDtypeStruct(w_down.shape, bf16),
        ]
        + sent_to
        + hidden_shapes,
        (),
        fetched=(grad, route_expert, route_slot, gates, saved_pre, w_down),
        scratch=[
            pltpu.VMEM(grad.shape, bf16),
            pltpu.VMEM(route_expert.shape, jnp.int32),
            pltpu.VMEM(route_slot.shape, jnp.int32),
            pltpu.VMEM(gates.shape, f32),
            pltpu.VMEM((hidden_width, ROUNDS * rows), bf16),
            pltpu.SemaphoreType.DMA((6,)),
        ],
        moved=3 * tokens * width * 2,
    )
    sent, hidden = made[: len(sent_to)], made[len(sent_to) :]
    if not packed:
        mine = lax.axis_index("edp")
        hidden = [
            lax.dynamic_slice_in_dim(hidden[0], (mine ^ step) * block, block, 0)
            for step in range(replicas)
        ]
    return table, sent, stored, down, hidden


def bring(value, after):
    def body(value_in, value_ref, sems):
        for copy in fetch(((value_in, value_ref),), sems):
            copy.wait()

    return on_chip(
        body,
        [jax.ShapeDtypeStruct(value.shape, value.dtype)],
        (),
        fetched=(value,),
        after=after,
        scratch=[pltpu.SemaphoreType.DMA((1,))],
        moved=2 * value.size,
    )[0]


def expert_rows(
    pieces_in, saved_pre, w_gate_up, w_down, round_index, senders, capacity, pairs=False, after=()
):
    rows = senders * capacity
    hidden_width, width = w_down.shape

    def body(stored_ref, up_ref, down_ref, *refs):
        in_refs, out_refs = refs[: len(pieces_in)], refs[len(pieces_in) :]
        routed = collect(in_refs, capacity)
        hidden_grad = dot(routed, down_ref[...], 1, 1)
        stored = stored_rows(stored_ref, round_index, senders, capacity)
        gate_pre, up_value = stored[:, :hidden_width], stored[:, hidden_width:]
        gate = 1.0 / (1.0 + jnp.exp(-gate_pre))
        act_grad = jnp.concatenate(
            [
                hidden_grad * up_value * gate * (1.0 + gate_pre * (1.0 - gate)),
                hidden_grad * gate_pre * gate,
            ],
            axis=1,
        ).astype(bf16)
        spread(dot(act_grad, up_ref[...], 1, 1), out_refs, capacity)

    return on_chip(
        body,
        sent_shapes(senders, capacity, width, pairs),
        (saved_pre, w_gate_up, w_down, *pieces_in),
        after=after,
        flops=6 * rows * hidden_width * width,
        moved=6 * hidden_width * width,
    )


def norm_backward(grad_out, branch, saved, gain):
    normed_in = saved.astype(f32)
    inverse = lax.rsqrt(jnp.mean(normed_in * normed_in, axis=1, keepdims=True) + NORM_EPS)
    scaled_in = normed_in * inverse
    norm_grad = branch * gain
    result = grad_out.astype(f32) + inverse * (
        norm_grad - scaled_in * jnp.mean(norm_grad * scaled_in, axis=1, keepdims=True)
    )
    return result.astype(bf16)


def first_combine(
    returned, grad, tail, saved_input, gain, route_expert, route_slot, table, capacity, senders, after=()
):
    tokens, width = grad.shape
    rows = senders * capacity
    pieces = len(returned)

    def body(grad_ref, tail_ref, saved_ref, gain_ref, expert_ref, slot_ref, table_ref, *refs):
        in_refs, (result_ref, *out_refs) = refs[:pieces], refs[pieces:]
        target = target_of(expert_ref[0, 0], slot_ref[0, 0], capacity)
        branch = dot(one_hot(target, rows), collect(in_refs, capacity), 0, 0)
        result = norm_backward(grad_ref[...], branch, saved_ref[0, 0], gain_ref[...])
        result_ref[...] = result
        first = lax.axis_index("pipe") == 0
        passed = jnp.where(first, tail_ref[...].astype(f32), result.astype(f32))
        later = table_ref[0:1, :].astype(jnp.int32)
        spread(dispatch_rows(passed, table_ref[1:2, :], later, rows), out_refs, capacity)

    result, *sent = on_chip(
        body,
        [jax.ShapeDtypeStruct((tokens, width), bf16)]
        + sent_shapes(senders, capacity, width),
        (grad, tail, saved_input, gain, route_expert, route_slot, table, *returned),
        after=after,
        moved=8 * tokens * width * 2,
    )
    return result, sent


def second_combine(
    returned, first_out, passed, tail, saved_input, gain, route_expert, route_slot, capacity, senders, after=()
):
    tokens, width = first_out.shape
    rows = senders * capacity
    pieces = len(returned)

    def body(first_ref, passed_ref, tail_ref, saved_ref, gain_ref, expert_ref, slot_ref, *refs):
        in_refs, (out_ref, token_ref) = refs[:pieces], refs[pieces:]
        token_ref[...] = jnp.zeros_like(token_ref)
        out_ref[0, 0] = first_ref[...]
        target = target_of(expert_ref[0, 1], slot_ref[0, 1], capacity)
        branch = dot(one_hot(target, rows), collect(in_refs, capacity), 0, 0)
        last = lax.axis_index("pipe") == lax.axis_size("pipe") - 1
        grad = jnp.where(last, tail_ref[...].astype(f32), passed_ref[...].astype(f32))
        out_ref[0, 1] = norm_backward(grad, branch, saved_ref[0, 1], gain_ref[...])

    return on_chip(
        body,
        [
            jax.ShapeDtypeStruct((1, ROUNDS, tokens, width), bf16),
            jax.ShapeDtypeStruct((8, 128), f32),
        ],
        (first_out, passed, tail, saved_input, gain, route_expert, route_slot, *returned),
        after=after,
        moved=8 * tokens * width * 2,
    )


def weight_grad(terms, rows, block, scale=None, earlier=None, after=()):
    width = terms[0][3].shape[1]
    arrays = []
    for term in terms:
        for array in (term[0], term[3]):
            if not any(array is other for other in arrays):
                arrays.append(array)

    def place(array):
        return next(index for index, other in enumerate(arrays) if other is array)

    sends = earlier is not None and block % 8 == 0 and width % 256 == 0
    parts = width // 256
    part = 256
    places = [(place(left), start, number, place(right)) for left, start, number, right in terms]

    def body(*refs):
        lefts, rights = [], []
        for left, start, number, right in places:
            columns = slice(number * rows, (number + 1) * rows)
            if start is None:
                lefts.append(refs[left][:, columns])
            else:
                lefts.append(unpack(refs[left], start, block, columns))
            rights.append(refs[right][0:rows, :])
        left_value = jnp.concatenate(lefts, axis=1)
        right_value = jnp.concatenate(rights, axis=0)
        if not sends:
            total = dot(left_value, right_value, 1, 0)
            if earlier is not None:
                total = (refs[len(arrays)][0, 0] + total) / scale
            refs[-1][0, 0] = total
            return
        out_ref, held, sems = refs[-3:]
        copies = []
        for index in range(parts):
            columns = slice(index * part, (index + 1) * part)
            total = dot(left_value, right_value[:, columns], 1, 0)
            held[:, columns] = (refs[len(arrays)][0, 0, :, columns] + total) / scale
            copies.append(
                pltpu.make_async_copy(
                    held.at[:, pl.ds(index * part, part)],
                    out_ref.at[0, 0, :, pl.ds(index * part, part)],
                    sems.at[index],
                )
            )
            copies[-1].start()
        for copy in copies:
            copy.wait()

    return on_chip(
        body,
        [jax.ShapeDtypeStruct((1, 1, block, width), f32)],
        tuple(arrays) + (() if earlier is None else (earlier,)),
        after=after,
        scratch=[pltpu.VMEM((block, width), f32), pltpu.SemaphoreType.DMA((parts,))]
        if sends
        else (),
        sends=sends,
        flops=2 * len(terms) * rows * block * width,
        moved=8 * block * width,
    )[0]


def at_distance(value, axis, step):
    count = lax.axis_size(axis)
    return lax.ppermute(value, axis, [(source, source ^ step) for source in range(count)])


def steps_over(axis, values):
    return [values[0]] + [
        at_distance(value, axis, step) for step, value in enumerate(values) if step
    ]


def behind(values):
    sections, count = lax.axis_size("pipe"), lax.axis_size("expert")
    return [
        lax.ppermute(
            value,
            ("pipe", "expert"),
            [
                (section * count + source, (section - 1) % sections * count + (source ^ step))
                for section in range(sections)
                for source in range(count)
            ],
        )
        for step, value in values
    ]


def local(
    head_grads,
    tail_grad,
    saved_input,
    norm_gain,
    route_expert,
    route_slot,
    gates,
    saved_pre,
    w_gate_up,
    w_down,
):
    senders = lax.axis_size("expert")
    replicas = lax.axis_size("edp")
    sections = lax.axis_size("pipe")
    rows = saved_pre.shape[3]
    capacity = rows // senders
    width = w_down.shape[3]
    hidden_width = w_down.shape[2]
    grad = head_grads[0]
    up, down = w_gate_up[0, 0], w_down[0, 0]

    def apart(parts):
        if len(parts) == senders:
            return parts
        return [parts[0][k * capacity : (k + 1) * capacity] for k in range(senders)]

    def together(parts, like):
        return parts if len(like) == senders else [jnp.concatenate(parts, axis=0)]

    def over_experts(parts, after=()):
        if even(senders, capacity) and len(parts) == 2:
            stays, turns = parts
            came = at_distance(turns, "expert", 1)
            (load,) = pair_up(stays, came, capacity, (1,), after)
            return [stays, came, at_distance(load, "expert", 2)]
        return together(steps_over("expert", apart(parts)), parts)

    def back(parts):
        return together(behind(list(enumerate(apart(parts)))), parts)

    route_expert, route_slot, gates = (
        jnp.transpose(value, (0, 1, 3, 2)) for value in (route_expert, route_slot, gates)
    )
    table, sent, stored, down, hidden = first_dispatch(
        grad,
        route_expert,
        route_slot,
        gates,
        saved_pre,
        down,
        capacity,
        senders,
        replicas,
    )
    up = bring(up, after=(table,))
    table = lax.ppermute(
        table, "pipe", [(source, (source + 1) % sections) for source in range(sections)]
    )
    arrived = over_experts(sent)
    block = hidden_width // replicas
    if rides_along(block, rows, width, replicas):
        joined, (near_load,) = join(
            arrived, hidden[1:2], capacity, rows, after=(up, table)
        )
        far = at_distance(joined, "edp", 2)
        near = at_distance(near_load, "edp", 1)
        arrived = [joined]
        early = (near, far)
        arrived = [joined]
    else:
        left = steps_over("edp", hidden)
        right = steps_over("edp", arrived * replicas)
        early = ()
    sent = expert_rows(
        arrived, stored, up, down, 0, senders, capacity
    )
    returned = over_experts(sent)
    first_out, sent = first_combine(
        returned,
        grad,
        tail_grad,
        saved_input,
        norm_gain,
        route_expert,
        route_slot,
        table,
        capacity,
        senders,
        after=early,
    )
    if early:
        last = at_distance(first_rows_of(far, rows, (sent[0],)), "edp", 1)
    arrived = back(sent)
    passed = lax.ppermute(
        first_out, "pipe", [(source, (source - 1) % sections) for source in range(sections)]
    )
    if rides_along(block, rows, width, replicas):
        again, _ = join(arrived, (), capacity, rows)
        second = at_distance(again, "edp", 2)
        first = at_distance(again, "edp", 1)
        third = at_distance(second, "edp", 1)
        units = [at_distance(hidden[step], "edp", step) for step in (2, 3)]
        arrived, late, tail = [again], (last,), (first, passed)
        now = [
            (hidden[0], 0, 0, joined),
            (near, rows, 0, near),
            (units[0], 0, 0, far),
            (hidden[0], 0, 1, again),
            (near, rows, 1, first),
            (units[0], 0, 1, second),
        ]
        then = [(units[1], 0, 0, last), (units[1], 0, 1, third)]
    else:
        late = tail = ()
        again = steps_over("edp", arrived * replicas)
        now = [(units, None, 0, value) for units, value in zip(left, right)]
        then = [(units, None, 1, value) for units, value in zip(left, again)]
    first_share = weight_grad(now, rows, block)
    returned = over_experts(
        expert_rows(
            arrived, stored, up, down, 1, senders, capacity, pairs=True, after=late
        ),
        after=tail,
    )
    input_out, done = second_combine(
        returned,
        first_out,
        passed,
        tail_grad,
        saved_input,
        norm_gain,
        route_expert,
        route_slot,
        capacity,
        senders,
        after=(first_share,),
    )
    grad_shard = weight_grad(
        then, rows, block, scale=float(replicas * ROUNDS), earlier=first_share, after=(done,)
    )
    return (input_out, grad_shard)


def solution(mesh):
    return jax.shard_map(
        local,
        mesh=mesh,
        in_specs=(
            P("pipe", ("expert", "edp"), None),
            P(("expert", "edp"), None),
            P("pipe", None, ("expert", "edp"), None),
            P("pipe", None),
            P("pipe", None, ("expert", "edp"), None),
            P("pipe", None, ("expert", "edp"), None),
            P("pipe", None, ("expert", "edp"), None),
            P("pipe", None, "expert", "edp", None),
            P("pipe", "expert", None, None),
            P("pipe", "expert", None, None),
        ),
        out_specs=(P("pipe", None, ("expert", "edp"), None), P("pipe", "expert", "edp", None)),
        check_vma=False,
    )
```
